32 devices in a mesh: group: 2 (over x), tm: 16 (over z, y, core).
Axes of the slice: x: 2, y: 2, z: 4, core: 2. Of those that a mesh axis runs over, the one named last changes fastest.
Arguments:
- noise: float32 [8, 4096], P('group'), parts along dimension 0, may hold values from -6 to 6
- labels: int32 [8], P('group'), parts along dimension 0, may hold values from 0 to 1000
- timesteps: int32 [25], replicated, may hold values from 0 to 399, as said below
- window_start: int32 [1], replicated, may hold values from 0 to 8
- time_weight_in: bfloat16 [256, 768], replicated, may hold values from -0.375 to 0.375
- time_weight_out: bfloat16 [768, 768], replicated, may hold values from -0.21875 to 0.21875
- class_table: bfloat16 [1001, 768], replicated, may hold values from -6 to 6
- patch_weight: bfloat16 [64, 768], replicated, may hold values from -0.75 to 0.75
- query_key_value: bfloat16 [1, 768, 2304], P(None, None, 'tm'), may hold values from -0.21875 to 0.21875
- mix_weight: bfloat16 [1, 768, 768], P(None, None, 'tm'), may hold values from -0.21875 to 0.21875
- expand_weight: bfloat16 [1, 768, 3072], P(None, None, 'tm'), may hold values from -0.21875 to 0.21875
- shrink_weight: bfloat16 [1, 3072, 768], P(None, None, 'tm'), may hold values from -0.109375 to 0.109375
- block_modulation: bfloat16 [1, 768, 4608], P(None, None, 'tm'), may hold values from -0.21875 to 0.21875
- final_modulation: bfloat16 [768, 1536], P(None, 'tm'), may hold values from -0.21875 to 0.21875
- output_weight: bfloat16 [768, 64], replicated, may hold values from -0.21875 to 0.21875
Outputs:
- trajectory: float32 [16, 8, 4096], P('tm', 'group'), parts along dimension 1
The draws below stay inside these ranges and needn't reach their ends.
There are 2 independent parts, one for each index of `group`. The reference program is written for one: setup_inputs(seed, part) draws one part's arguments, and reference() takes and returns one part's arrays. A program takes and returns all parts, laid end to end along the dimension named above; an argument that names none is the same for every part. Nothing has to cross between parts.
Inputs may be any that keep to these rules, and one draw needn't show every extreme that they name: `timesteps`: strictly decreasing; the first entry is 399 and the last is 0.
All inputs are finite; a program needn't handle non-finite values.
Results may differ from the reference program's by a relative error of at most 0.0025.
Values may be sent and summed in bfloat16 or wider, within the bound.
No kernel may reach another device: no remote copies, remote signals or barrier semaphores. Data moves between devices by JAX's collectives and lax.ppermute only.
A program may use at most 128 MiB of HBM per device.

```python
import math
import jax
import jax.numpy as jnp
from jax import lax

D = 768
FF = 3072
HEADS = 12
PATCH_DIM = 64
CLASSES = 1000
FREQ = 256
SAMPLES = 4
LAYERS = 1
ITERS = 2
TRAIN_T = 1000
SPAN = 400
EXTRA = 8
LATENT = 4096
STEPS = 16
SCHED = 25


def draw_timesteps(key, part):
    inner = jax.random.permutation(key, SPAN - 2)[:SCHED - 2] + 1
    ordered = -jnp.sort(-inner)
    first = jnp.full((1,), SPAN - 1, dtype=jnp.int32)
    last = jnp.zeros((1,), dtype=jnp.int32)
    return jnp.concatenate([first, ordered.astype(jnp.int32), last])


def touch_ends(values, stream_key, smallest, high):
    longest = values.shape.index(max(values.shape))
    spots = []
    for shift in (0, 1):
        where = [jax.random.randint(jax.random.fold_in(stream_key, axis), (), 0, length) for axis, length in enumerate(values.shape)]
        where[longest] = (where[longest] + shift) % values.shape[longest]
        spots.append(tuple(where))
    return values.at[spots[0]].set(smallest).at[spots[1]].set(high)


def steps_of(own_key, dims, split, smallest, high):
    gain, own = 1.0, jax.random.fold_in(own_key, 6)
    for dim, blocks in split:
        heights = jnp.exp(jax.random.uniform(jax.random.fold_in(own, dim), (blocks,), jnp.float32, smallest / len(split), high / len(split)))
        gain = gain * jnp.repeat(heights, dims[dim] // blocks).reshape([-1 if axis == dim else 1 for axis in range(len(dims))])
    return gain


def gaussian(own_key, shape, spread, bound, split=(), kind=jnp.bfloat16):
    values = jax.random.normal(own_key, shape, jnp.float32) * spread
    if len(split) > 0:
        values = steps_of(own_key, shape, split, -0.22, 0.18) * values
    return jnp.clip(values, min=-bound, max=bound).astype(kind)


def setup_inputs(seed: int = 0, part: int = 0) -> dict:
    arg_keys = jax.random.split(jax.random.key(seed), 16)
    part_keys = jax.random.split(jax.random.fold_in(arg_keys[15], part), 16)
    noise = gaussian(part_keys[0], (SAMPLES, LATENT), 1.0, 6.0, (), jnp.float32)
    labels = touch_ends(jax.random.randint(part_keys[1], (SAMPLES,), 0, CLASSES + 1), jax.random.fold_in(part_keys[1], 1), 0, CLASSES).astype(jnp.int32)
    timesteps = draw_timesteps(jax.random.fold_in(arg_keys[15], 71), part)
    window_start = jax.random.randint(arg_keys[3], (1,), 0, EXTRA + 1).astype(jnp.int32)
    time_weight_in = gaussian(arg_keys[4], (FREQ, D), FREQ ** -0.5, 0.375)
    time_weight_out = gaussian(arg_keys[5], (D, D), D ** -0.5, 0.21875)
    class_table = gaussian(arg_keys[6], (CLASSES + 1, D), 1.0, 6.0)
    patch_weight = gaussian(arg_keys[7], (PATCH_DIM, D), PATCH_DIM ** -0.5, 0.75)
    query_key_value = gaussian(arg_keys[8], (LAYERS, D, 3 * D), D ** -0.5, 0.21875, ((2, 16),))
    mix_weight = gaussian(arg_keys[9], (LAYERS, D, D), D ** -0.5, 0.21875, ((2, 16),))
    expand_weight = gaussian(arg_keys[10], (LAYERS, D, FF), D ** -0.5, 0.21875, ((2, 16),))
    shrink_weight = gaussian(arg_keys[11], (LAYERS, FF, D), FF ** -0.5, 0.109375, ((2, 16),))
    block_modulation = gaussian(arg_keys[12], (LAYERS, D, 6 * D), D ** -0.5, 0.21875, ((2, 16),))
    final_modulation = gaussian(arg_keys[13], (D, 2 * D), D ** -0.5, 0.21875, ((1, 16),))
    output_weight = gaussian(arg_keys[14], (D, PATCH_DIM), D ** -0.5, 0.21875)
    return dict(noise=noise, labels=labels, timesteps=timesteps, window_start=window_start, time_weight_in=time_weight_in, time_weight_out=time_weight_out, class_table=class_table, patch_weight=patch_weight, query_key_value=query_key_value, mix_weight=mix_weight, expand_weight=expand_weight, shrink_weight=shrink_weight, block_modulation=block_modulation, final_modulation=final_modulation, output_weight=output_weight)


def layer_norm(values):
    average = lax.optimization_barrier(jnp.mean(values, axis=-1, keepdims=True))
    centered = values - average
    variance = lax.optimization_barrier(jnp.mean(centered * centered, axis=-1, keepdims=True))
    return centered / jnp.sqrt(variance + 1e-06)

def position_table(count, width):
    side = math.isqrt(count)
    quarter = width // 4
    omega = 1.0 / 10000.0 ** (jnp.arange(quarter, dtype=jnp.float32) / quarter)
    index = jnp.arange(count, dtype=jnp.int32)
    first = (index // side).astype(jnp.float32)[:, None] * omega[None, :]
    second = (index % side).astype(jnp.float32)[:, None] * omega[None, :]
    return jnp.concatenate([jnp.sin(first), jnp.cos(first), jnp.sin(second), jnp.cos(second)], axis=1)

def plan_terms(timesteps, window_start, step_index, train_steps):
    levels = jnp.arange(train_steps, dtype=jnp.float32)
    betas = 0.0001 + (0.02 - 0.0001) * levels / (train_steps - 1)
    alpha_bar = jnp.cumprod(1.0 - betas)
    current = jnp.take(timesteps, window_start[0] + step_index)
    following = jnp.take(timesteps, window_start[0] + step_index + 1)
    bar_current = jnp.take(alpha_bar, current)
    bar_following = jnp.take(alpha_bar, following)
    scale_state = jnp.sqrt(bar_following / bar_current)
    scale_noise = jnp.sqrt(1.0 - bar_following) - scale_state * jnp.sqrt(1.0 - bar_current)
    return (current, scale_state, scale_noise)

def conditioning(current, labels, time_weight_in, time_weight_out, class_table):
    half = time_weight_in.shape[0] // 2
    rates = jnp.exp(-math.log(10000.0) * jnp.arange(half, dtype=jnp.float32) / half)
    angles = current.astype(jnp.float32)[:, None] * rates[None, :]
    features = jnp.concatenate([jnp.cos(angles), jnp.sin(angles)], axis=1).astype(jnp.bfloat16)
    time_hidden = jax.nn.silu(jnp.dot(features, time_weight_in, preferred_element_type=jnp.float32)).astype(jnp.bfloat16)
    time_embed = jnp.dot(time_hidden, time_weight_out, preferred_element_type=jnp.float32)
    selector = (labels[:, None] == jnp.arange(class_table.shape[0], dtype=jnp.int32)[None, :]).astype(jnp.bfloat16)
    class_embed = jnp.dot(selector, class_table, preferred_element_type=jnp.float32)
    return jax.nn.silu(time_embed[:, None, :] + class_embed[None, :, :]).astype(jnp.bfloat16)

def network(states, block_terms, final_terms, patch_weight, query_key_value, mix_weight, expand_weight, shrink_weight, output_weight, heads):
    count = states.shape[0]
    patch = patch_weight.shape[0]
    width = patch_weight.shape[1]
    tokens = states.shape[1] // patch
    head_dim = width // heads
    patches = states.reshape(count * tokens, patch).astype(jnp.bfloat16)
    hidden = jnp.dot(patches, patch_weight, preferred_element_type=jnp.float32).reshape(count, tokens, width)
    hidden = hidden + position_table(tokens, width)[None]
    for layer in range(block_terms.shape[0]):
        blocks = block_terms[layer].reshape(count, 6, 1, width)
        normed = (layer_norm(hidden) * (1.0 + blocks[:, 1]) + blocks[:, 0]).astype(jnp.bfloat16)
        projected = jnp.dot(normed.reshape(count * tokens, width), query_key_value[layer], preferred_element_type=jnp.float32).astype(jnp.bfloat16)
        projected = projected.reshape(count, tokens, 3, heads, head_dim).astype(jnp.float32)
        scores = jnp.einsum('rqhd,rkhd->rhqk', projected[:, :, 0], projected[:, :, 1]) / math.sqrt(head_dim)
        raised = jnp.exp(scores)
        weights = (raised / lax.optimization_barrier(jnp.sum(raised, axis=-1, keepdims=True))).astype(jnp.bfloat16)
        attended = jnp.einsum('rhqk,rkhd->rqhd', weights.astype(jnp.float32), projected[:, :, 2]).astype(jnp.bfloat16)
        mixed = jnp.dot(attended.reshape(count * tokens, width), mix_weight[layer], preferred_element_type=jnp.float32)
        hidden = hidden + blocks[:, 2] * mixed.reshape(count, tokens, width)
        normed = (layer_norm(hidden) * (1.0 + blocks[:, 4]) + blocks[:, 3]).astype(jnp.bfloat16)
        expanded = jax.nn.gelu(jnp.dot(normed.reshape(count * tokens, width), expand_weight[layer], preferred_element_type=jnp.float32), approximate=True).astype(jnp.bfloat16)
        shrunk = jnp.dot(expanded, shrink_weight[layer], preferred_element_type=jnp.float32)
        hidden = hidden + blocks[:, 5] * shrunk.reshape(count, tokens, width)
    final = final_terms.reshape(count, 2, 1, width)
    normed = (layer_norm(hidden) * (1.0 + final[:, 1]) + final[:, 0]).astype(jnp.bfloat16)
    return jnp.dot(normed.reshape(count * tokens, width), output_weight, preferred_element_type=jnp.float32).reshape(count, tokens * patch)

def reference(noise, labels, timesteps, window_start, time_weight_in, time_weight_out, class_table, patch_weight, query_key_value, mix_weight, expand_weight, shrink_weight, block_modulation, final_modulation, output_weight):
    step_index = jnp.arange(STEPS, dtype=jnp.int32)
    current, scale_state, scale_noise = plan_terms(timesteps, window_start, step_index, TRAIN_T)
    condition = conditioning(current, labels, time_weight_in, time_weight_out, class_table)

    def one_step(item):
        rows, acting = item
        block_terms = jnp.einsum('rd,ldc->lrc', acting.astype(jnp.float32), block_modulation.astype(jnp.float32))
        final_terms = jnp.dot(acting, final_modulation, preferred_element_type=jnp.float32)
        return network(rows, block_terms, final_terms, patch_weight, query_key_value, mix_weight, expand_weight, shrink_weight, output_weight, HEADS)
    states = jnp.broadcast_to(noise[None], (STEPS,) + noise.shape)
    running = states
    for sweep in range(ITERS):
        predicted = lax.map(one_step, (states, condition))
        drift = (scale_state - 1.0)[:, None, None] * states + scale_noise[:, None, None] * predicted
        running = jnp.cumsum(drift, axis=0)
        states = noise[None] + running - drift
    return noise[None] + running
```

```python
import functools
import math

import jax
import jax.numpy as jnp
from jax import lax
from jax.experimental import pallas as pl
from jax.experimental.pallas import tpu as pltpu
from jax.sharding import PartitionSpec as P

HEADS = 12
ITERS = 2
TRAIN_T = 1000
WINDOW = 5
BF16 = jnp.bfloat16
F32 = jnp.float32


def plan_terms(timesteps, window_start, step_index, train_steps):
    levels = jnp.arange(train_steps, dtype=F32)
    betas = 0.0001 + (0.02 - 0.0001) * levels / (train_steps - 1)
    alpha_bar = jnp.cumprod(1.0 - betas)
    current = jnp.take(timesteps, window_start[0] + step_index)
    following = jnp.take(timesteps, window_start[0] + step_index + 1)
    bar_current = jnp.take(alpha_bar, current)
    bar_following = jnp.take(alpha_bar, following)
    scale_state = jnp.sqrt(bar_following / bar_current)
    scale_noise = jnp.sqrt(1.0 - bar_following) - scale_state * jnp.sqrt(1.0 - bar_current)
    return (current, scale_state, scale_noise)


def conditioning(current, labels, time_weight_in, time_weight_out, class_table):
    half = time_weight_in.shape[0] // 2
    rates = jnp.exp(-math.log(10000.0) * jnp.arange(half, dtype=F32) / half)
    angles = current.astype(F32)[:, None] * rates[None, :]
    features = jnp.concatenate([jnp.cos(angles), jnp.sin(angles)], axis=1).astype(BF16)
    time_hidden = jax.nn.silu(
        jnp.dot(features, time_weight_in, preferred_element_type=F32)
    ).astype(BF16)
    time_embed = jnp.dot(time_hidden, time_weight_out, preferred_element_type=F32)
    selector = (
        labels[:, None] == jnp.arange(class_table.shape[0], dtype=jnp.int32)[None, :]
    ).astype(BF16)
    class_embed = jnp.dot(selector, class_table, preferred_element_type=F32)
    return jax.nn.silu(time_embed[:, None, :] + class_embed[None, :, :]).astype(BF16)


def position_columns(count, width):
    side = math.isqrt(count)
    quarter = width // 4
    omega = 1.0 / 10000.0 ** (jnp.arange(quarter, dtype=F32) / quarter)
    index = jnp.arange(count, dtype=jnp.int32)
    first = omega[:, None] * (index // side).astype(F32)[None, :]
    second = omega[:, None] * (index % side).astype(F32)[None, :]
    return jnp.concatenate(
        [jnp.sin(first), jnp.cos(first), jnp.sin(second), jnp.cos(second)], axis=0
    )


def ring_order(count):
    return list(range(0, count, 2)) + list(range(1, count, 2))[::-1]


class Mover:
    def __init__(self, groups, count):
        self.groups, self.count, self.sent = groups, count, []

    def swap(self, value, distance):
        return self._send(value, lambda i: i ^ distance, lambda g: g)

    def across(self, value):
        return self._send(value, lambda i: i, lambda g: g ^ 1)

    def ring(self, value):
        order = ring_order(self.count // 4)
        after = {z: order[(k + 1) % len(order)] for k, z in enumerate(order)}
        return self._send(value, lambda i: after[i // 4] * 4 + i % 4, lambda g: g)

    def _send(self, value, target, side):
        if len(self.sent) >= WINDOW:
            value, _ = lax.optimization_barrier((value, self.sent[-WINDOW]))
        pairs = [
            (g * self.count + i, side(g) * self.count + target(i))
            for g in range(self.groups)
            for i in range(self.count)
        ]
        value = lax.ppermute(value, ("group", "tm"), pairs)
        self.sent.append(value)
        return value


def spread_weights(first, second, groups, count):
    mover = Mover(groups, count)
    depth = count // 4
    p, h = first.shape[0], second.shape[1]
    side = lax.axis_index("group")
    mine = jnp.where(side == 0, second[0], second[1])
    held = {("p", 0, 0): first, ("h", 0, 0): mine}
    first_out, second_out = [], []
    everything = jnp.concatenate([first, second[0], second[1]], axis=0)

    def z(kind, r):
        held[kind, r, 0] = mover.ring(held[kind, r - 1, 0])

    def y(kind, r):
        held[kind, r, 1] = mover.swap(held[kind, r, 0], 2)

    stacks = {}

    def x(j, keys):
        stack = jnp.concatenate([held[k] for k in keys], axis=0)
        stacks[j] = (keys, stack, mover.across(stack))

    def core_second(j):
        keys, stack, other = stacks[j]
        buffer = jnp.concatenate([stack, other], axis=0)
        received = mover.swap(buffer, 1)
        for core, data in ((0, buffer), (1, received)):
            pieces = []
            for half in range(2):
                for k, (_, r, dy) in enumerate(keys):
                    pieces.append(((half * len(keys) + k) * h, r, dy, core, half))
            second_out.append((data, pieces))

    def core_first(keys):
        buffer = jnp.concatenate([held[k] for k in keys], axis=0)
        received = mover.swap(buffer, 1)
        for core, data in ((0, buffer), (1, received)):
            pieces = [(k * p, r, dy, core, 0) for k, (_, r, dy) in enumerate(keys)]
            first_out.append((data, pieces))

    def core_own():
        received = mover.swap(everything, 1)
        for core, data in ((0, everything), (1, received)):
            first_out.append((data, [(0, 0, 0, core, 0)]))
            second_out.append((data, [(p, 0, 0, core, "lo"), (p + h, 0, 0, core, "hi")]))

    group = lambda j: [("h", j + 1, 0), ("h", j, 1)] if j + 1 < depth else [("h", j, 1)]
    z("p", 1), y("p", 0), z("h", 1), y("h", 0), core_own()
    z("p", 2), x(0, group(0)), y("p", 1), z("h", 2), y("h", 1)
    z("p", 3), y("p", 2), x(1, group(1)), z("h", 3)
    core_first([("p", 1, 0), ("p", 0, 1), ("p", 1, 1)])
    y("h", 2), y("p", 3), core_second(0), x(2, group(2))
    core_first([("p", 2, 0), ("p", 3, 0), ("p", 2, 1), ("p", 3, 1)])
    y("h", 3), core_second(1), x(3, group(3)), core_second(2), core_second(3)
    return first_out, second_out


def piece_owners(count):
    position = lax.axis_index("tm")
    depth = count // 4
    order = ring_order(depth)
    place = jnp.asarray([order.index(z) for z in range(depth)], jnp.int32)[position // 4]
    rows = []
    for r in range(depth):
        z = jnp.asarray(order, jnp.int32)[(place - r + depth) % depth]
        for dy in range(2):
            for core in range(2):
                rows.append(z * 4 + ((position % 4) ^ (2 * dy + core)))
    return jnp.stack(rows).astype(jnp.int32)


def norm(hidden, shift, scale):
    average = jnp.mean(hidden, axis=0, keepdims=True)
    centered = hidden - average
    variance = jnp.mean(centered * centered, axis=0, keepdims=True)
    return (centered * lax.rsqrt(variance + 1e-06) * (1.0 + scale) + shift).astype(BF16)


def dims_of(terms, tokens, samples):
    return samples, tokens // samples


def spread_terms(terms_ref, which, width, tokens, samples):
    each = tokens // samples
    rows = terms_ref.shape[0]
    own = lax.broadcasted_iota(jnp.int32, (rows, tokens), 0)
    of = lax.broadcasted_iota(jnp.int32, (rows, tokens), 1) // each
    pick = jnp.where(own == of, 1.0, 0.0).astype(BF16)
    return lax.dot_general(
        terms_ref[:, which * width : (which + 1) * width],
        pick,
        (((0,), (0,)), ((), ())),
        preferred_element_type=F32,
    )


def attention_part(state_ref, patch_ref, place_ref, terms_ref, wq, wm, qkv, att, ready, heads, samples):
    width, tokens = place_ref.shape
    each = tokens // samples
    size = width // heads
    terms = lambda k: spread_terms(terms_ref, k, width, tokens, samples)
    hidden = (
        jnp.dot(patch_ref[...], state_ref[...].astype(BF16), preferred_element_type=F32)
        + place_ref[...]
    )
    normed = norm(hidden, terms(0), terms(1))
    ready[0]()
    for k in range(3):
        rows = pl.ds(k * width, width)
        qkv[rows, :] = jnp.dot(wq[rows, :], normed, preferred_element_type=F32).astype(BF16)
    sample_of = lax.broadcasted_iota(jnp.int32, (each, tokens), 1) // each
    scale = 1.0 / math.sqrt(size)
    for k in range(heads):
        query = qkv[pl.ds(k * size, size), :]
        key = qkv[pl.ds(width + k * size, size), :]
        value = qkv[pl.ds(2 * width + k * size, size), :]
        scores = lax.dot_general(
            key, query, (((0,), (0,)), ((), ())), preferred_element_type=F32
        )
        mine = scores[0:each]
        for s in range(1, samples):
            mine = jnp.where(sample_of == s, scores[s * each : (s + 1) * each], mine)
        raised = jnp.exp(mine * scale)
        weights = (raised / jnp.sum(raised, axis=0, keepdims=True)).astype(F32)
        spread = jnp.concatenate(
            [jnp.where(sample_of == s, weights, 0.0).astype(BF16) for s in range(samples)], axis=0
        )
        att[pl.ds(k * size, size), :] = jnp.dot(
            value, spread, preferred_element_type=F32
        ).astype(BF16)
    ready[1]()
    mixed = jnp.dot(wm[...], att[...], preferred_element_type=F32)
    return hidden + terms(2) * mixed


def feed_part(hidden, state_ref, terms_ref, out_ref, scalars_ref, we, ws, mid, ready, samples):
    width, tokens = hidden.shape
    terms = lambda k: spread_terms(terms_ref, k, width, tokens, samples)
    normed = norm(hidden, terms(3), terms(4))
    ready[2]()
    for k in range(we.shape[0] // width):
        rows = pl.ds(k * width, width)
        mid[rows, :] = jax.nn.gelu(
            jnp.dot(we[rows, :], normed, preferred_element_type=F32), approximate=True
        ).astype(BF16)
    ready[3]()
    shrunk = jnp.zeros_like(hidden)
    for k in range(we.shape[0] // width):
        rows = pl.ds(k * width, width)
        shrunk = shrunk + jnp.dot(ws[rows, :], mid[rows, :], preferred_element_type=F32)
    hidden = hidden + terms(5) * shrunk
    normed = norm(hidden, terms(6), terms(7))
    predicted = jnp.dot(out_ref[...], normed, preferred_element_type=F32)
    return (scalars_ref[0] - 1.0) * state_ref[...] + scalars_ref[1] * predicted


def network_kernel(parts, sources, sizes, heads, samples, *refs):
    nq, nm, ne, ns, width = sizes
    refs = list(refs)
    take = lambda: refs.pop(0)
    owners, scalars, state, patch, place, terms, out_weight = (take() for _ in range(7))
    before = None if 0 in parts else take()
    buffers = [take() for _ in sources]
    results = [take() for _ in range(1 if 1 not in parts else 2)]
    if 0 in parts:
        wq, wm, qkv, att = (take() for _ in range(4))
    if 1 in parts:
        we, ws, mid = (take() for _ in range(3))
    sems = take()

    def copy(src, dst, k):
        pltpu.make_async_copy(src, dst, sems.at[k]).start()

    def at(ref, start, rows):
        return ref.at[pl.ds(pl.multiple_of(start, 16), rows), :]

    half_e, halves = ne // 2, ns // 2
    for stage in range(2):
        if stage not in parts:
            continue
        for ref, (stages, pieces) in zip(buffers, sources):
            if stages != stage:
                continue
            if pieces is None:
                continue
            for row, r, dy, core, half in pieces:
                shard = owners[(r * 2 + dy) * 2 + core]
                if stage == 0:
                    copy(ref.at[pl.ds(row, nq), :], at(wq, shard * nq, nq), 0)
                    copy(ref.at[pl.ds(row + nq, nm), :], at(wm, shard * nm, nm), 1)
                else:
                    side = owners[owners.shape[0] - 1]
                    side = {0: side, 1: 1 - side, "lo": 0, "hi": 1}[half]
                    copy(
                        ref.at[pl.ds(row, half_e), :], at(we, shard * ne + side * half_e, half_e), 2
                    )
                    for k in range(halves):
                        copy(
                            ref.at[pl.ds(row + half_e + k * nm, nm), :],
                            at(ws, (side * halves + k) * width + shard * nm, nm),
                            3,
                        )
    whole = [pieces for _, pieces in sources]
    if all(p is None for p in whole):
        targets = ([wq, wm] if 0 in parts else []) + ([we, ws] if 1 in parts else [])
        first = 0 if 0 in parts else 2
        for k, (ref, dst) in enumerate(zip(buffers, targets)):
            copy(ref, dst, first + k)

    def waiter(ref, k):
        return lambda: pltpu.make_async_copy(ref, ref, sems.at[k]).wait()

    ready = {}
    if 0 in parts:
        ready[0], ready[1] = waiter(wq, 0), waiter(wm, 1)
    if 1 in parts:
        ready[2], ready[3] = waiter(we, 2), waiter(ws, 3)
    if 0 in parts:
        hidden = attention_part(
            state, patch, place, terms, wq, wm, qkv, att, ready, heads, samples
        )
    else:
        hidden = before[...]
    if 1 not in parts:
        results[0][...] = hidden
        return
    drift = feed_part(hidden, state, terms, out_weight, scalars, we, ws, mid, ready, samples)
    results[0][...] = drift
    results[1][...] = drift.astype(BF16)


def run_network(parts, fixed, before, buffers, sizes, heads, samples):
    width, tokens = fixed[4].shape
    patch = fixed[2].shape[0]
    nq, nm, ne, ns, _ = sizes
    ff = ns * width
    smem = pl.BlockSpec(memory_space=pltpu.SMEM)
    vmem = pl.BlockSpec(memory_space=pltpu.VMEM)
    anywhere = pl.BlockSpec(memory_space=pl.ANY)
    scratch = []
    if 0 in parts:
        scratch += [
            pltpu.VMEM((3 * width, width), BF16),
            pltpu.VMEM((width, width), BF16),
            pltpu.VMEM((3 * width, tokens), BF16),
            pltpu.VMEM((width, tokens), BF16),
        ]
    if 1 in parts:
        scratch += [
            pltpu.VMEM((ff, width), BF16),
            pltpu.VMEM((ff, width), BF16),
            pltpu.VMEM((ff, tokens), BF16),
        ]
    scratch.append(pltpu.SemaphoreType.DMA((4,)))
    if 1 in parts:
        out_shape = [
            jax.ShapeDtypeStruct((patch, tokens), F32),
            jax.ShapeDtypeStruct((patch, tokens), BF16),
        ]
    else:
        out_shape = [jax.ShapeDtypeStruct((width, tokens), F32)]
    rows = (4 * width if 0 in parts else 0) + (2 * ff if 1 in parts else 0)
    extra = [] if before is None else [before]
    return pl.pallas_call(
        functools.partial(
            network_kernel, parts, [(s, p) for s, _, p in buffers], sizes, heads, samples
        ),
        out_shape=out_shape,
        in_specs=[smem, smem] + [vmem] * (len(fixed) - 2 + len(extra)) + [anywhere] * len(buffers),
        out_specs=[vmem] * len(out_shape),
        scratch_shapes=scratch,
        compiler_params=pltpu.CompilerParams(vmem_limit_bytes=40 * 1024 * 1024),
        cost_estimate=pl.CostEstimate(
            flops=2 * rows * width * tokens, bytes_accessed=2 * rows * width, transcendentals=0
        ),
    )(*fixed, *extra, *[b for _, b, _ in buffers])


def earlier_sum(value, narrow, count):
    position = lax.axis_index("tm")
    total = value
    before = jnp.zeros_like(value)
    distance = 1
    while distance < count:
        pairs = [(i, i ^ distance) for i in range(count)]
        other = lax.ppermute(narrow, "tm", pairs).astype(value.dtype)
        before = jnp.where((position & distance) != 0, before + other, before)
        total = total + other
        narrow = total.astype(BF16)
        distance *= 2
    return before


def body(
    noise,
    labels,
    timesteps,
    window_start,
    time_weight_in,
    time_weight_out,
    class_table,
    patch_weight,
    query_key_value,
    mix_weight,
    expand_weight,
    shrink_weight,
    block_modulation,
    final_modulation,
    output_weight,
):
    groups, count = lax.axis_size("group"), lax.axis_size("tm")
    samples, latent = noise.shape
    patch, width = patch_weight.shape
    each = latent // patch
    tokens = samples * each
    position = lax.axis_index("tm")

    nq, nm, ne = query_key_value.shape[2], mix_weight.shape[2], expand_weight.shape[2]
    ns = shrink_weight.shape[1] // width
    sizes = (nq, nm, ne, ns, width)
    q_rows, m_rows, e_rows = query_key_value[0].T, mix_weight[0].T, expand_weight[0].T
    s_rows = shrink_weight[0].reshape(ns, width, nm).transpose(0, 2, 1)
    short = (
        groups == 2
        and count == 16
        and ns % 2 == 0
        and all(v % 16 == 0 for v in (nq, nm, ne // 2))
    )
    if short:
        half_e, half_s = ne // 2, ns // 2
        first = jnp.concatenate([q_rows, m_rows], axis=0)
        second = jnp.stack(
            [
                jnp.concatenate(
                    [e_rows[k * half_e : (k + 1) * half_e]]
                    + [s_rows[k * half_s + j] for j in range(half_s)],
                    axis=0,
                )
                for k in range(2)
            ]
        )
        first_out, second_out = spread_weights(first, second, groups, count)
        owners = jnp.concatenate(
            [piece_owners(count), lax.axis_index("group").astype(jnp.int32)[None]]
        )
        first_buffers = [(0, data, pieces) for data, pieces in first_out]
        second_buffers = [(1, data, pieces) for data, pieces in second_out]
    else:
        whole = lambda rows, axis: lax.all_gather(rows, "tm", axis=axis, tiled=True)
        owners = jnp.zeros((1,), jnp.int32)
        first_buffers = [(0, whole(q_rows, 0), None), (0, whole(m_rows, 0), None)]
        second_buffers = [
            (1, whole(e_rows, 0), None),
            (1, whole(s_rows, 1).reshape(ns * width, width), None),
        ]

    steps = jnp.arange(count, dtype=jnp.int32)
    current, scale_state, scale_noise = plan_terms(timesteps, window_start, steps, TRAIN_T)
    scalars = jnp.stack([scale_state[position], scale_noise[position]])
    condition = conditioning(current, labels, time_weight_in, time_weight_out, class_table)
    rows = condition.reshape(count * samples, width)
    block_part = jnp.dot(rows, block_modulation[0], preferred_element_type=F32).astype(BF16)
    final_part = jnp.dot(rows, final_modulation, preferred_element_type=F32).astype(BF16)
    nb = block_part.shape[1]
    both = jnp.concatenate([block_part, final_part], axis=1).reshape(count, samples, -1)
    both = lax.all_to_all(both, "tm", split_axis=0, concat_axis=0, tiled=True)
    unfold = lambda t: t.transpose(1, 0, 2).reshape(samples, -1)
    terms = jnp.concatenate([unfold(both[:, :, :nb]), unfold(both[:, :, nb:])], axis=1)
    terms = jnp.pad(terms, ((0, -samples % 16), (0, 0)))

    start = noise.reshape(samples, each, patch).transpose(2, 0, 1).reshape(patch, tokens)
    place = jnp.tile(position_columns(each, width), (1, samples))
    patch_rows, out_rows = patch_weight.T, output_weight.T

    states = start
    for sweep in range(ITERS):
        fixed = (owners, scalars, states, patch_rows, place, terms, out_rows)
        if sweep == 0:
            (hidden,) = run_network((0,), fixed, None, first_buffers, sizes, HEADS, samples)
            drift, narrow = run_network(
                (1,), fixed, hidden, second_buffers, sizes, HEADS, samples
            )
        else:
            drift, narrow = run_network(
                (0, 1), fixed, None, first_buffers + second_buffers, sizes, HEADS, samples
            )
        before = earlier_sum(drift, narrow, count)
        running = before + drift
        states = start + before
    result = (start + running).reshape(patch, samples, each).transpose(1, 2, 0)
    return result.reshape(1, samples, latent)


def solution(mesh):
    return jax.shard_map(
        body,
        mesh=mesh,
        in_specs=(
            P("group", None),
            P("group"),
            P(),
            P(),
            P(),
            P(),
            P(),
            P(),
            P(None, None, "tm"),
            P(None, None, "tm"),
            P(None, None, "tm"),
            P(None, None, "tm"),
            P(None, None, "tm"),
            P(None, "tm"),
            P(),
        ),
        out_specs=P("tm", "group", None),
        check_vma=False,
    )
```

```python
import functools
import math

import jax
import jax.numpy as jnp
import numpy as np
from jax import lax
from jax.experimental import pallas as pl
from jax.experimental.pallas import tpu as pltpu
from jax.sharding import PartitionSpec as P

HEADS = 12
ITERS = 2
TRAIN_T = 1000
WINDOW = 5
CORE_COUNTS = False
PAD = 8
VMEM_LIMIT = 53 * 1024 * 1024
BF16 = jnp.bfloat16
F32 = jnp.float32


def noise_levels(train_steps):
    levels = np.arange(train_steps, dtype=np.float32)
    betas = np.float32(0.0001) + np.float32(0.02 - 0.0001) * levels / np.float32(train_steps - 1)
    return np.cumprod((np.float32(1.0) - betas).astype(np.float64)).astype(np.float32)


def position_columns(count, width, samples):
    side = math.isqrt(count)
    quarter = width // 4
    omega = 1.0 / 10000.0 ** (np.arange(quarter, dtype=np.float64) / quarter)
    index = np.arange(count)
    first = omega[:, None] * (index // side)[None, :]
    second = omega[:, None] * (index % side)[None, :]
    table = np.concatenate([np.sin(first), np.cos(first), np.sin(second), np.cos(second)], axis=0)
    return np.tile(table, (1, samples)).astype(np.float32)


def conditioning_kernel(
    steps, samples, times, window, levels, w_in, w_out, classes, blocks, finals, part, scales
):
    half = w_in.shape[0] // 2
    row = lax.broadcasted_iota(jnp.int32, (steps, half), 0)
    lane = lax.broadcasted_iota(jnp.int32, (steps, half), 1).astype(F32)
    place = lax.broadcasted_iota(jnp.int32, (steps, scales.shape[1]), 0)
    current = jnp.zeros((steps, half), F32)
    now = jnp.ones(place.shape, F32)
    then = jnp.ones(place.shape, F32)
    for j in range(steps):
        here, after = times[window[0] + j], times[window[0] + j + 1]
        current = jnp.where(row == j, here.astype(F32), current)
        now = jnp.where(place == j, levels[here], now)
        then = jnp.where(place == j, levels[after], then)
    scale = jnp.sqrt(then / now)
    scales[0:steps, :] = scale
    scales[steps : 2 * steps, :] = jnp.sqrt(1.0 - then) - scale * jnp.sqrt(1.0 - now)
    angles = current * jnp.exp(-math.log(10000.0) * lane / half)
    features = jnp.concatenate([jnp.cos(angles), jnp.sin(angles)], axis=1).astype(BF16)
    hidden = jax.nn.silu(jnp.dot(features, w_in[...], preferred_element_type=F32)).astype(BF16)
    embed = jnp.dot(hidden, w_out[...], preferred_element_type=F32)
    rows = jnp.concatenate(
        [jax.nn.silu(embed + classes[s : s + 1, :]).astype(BF16) for s in range(samples)], axis=0
    )
    to = lax.broadcasted_iota(jnp.int32, (rows.shape[0], rows.shape[0]), 0)
    of = lax.broadcasted_iota(jnp.int32, (rows.shape[0], rows.shape[0]), 1)
    turn = jnp.where(of == (to % samples) * steps + to // samples, 1.0, 0.0).astype(BF16)
    rows = jnp.dot(turn, rows, preferred_element_type=F32).astype(BF16)
    nb = blocks.shape[0]
    contract = (((1,), (1,)), ((), ()))
    part[:, 0:nb] = lax.dot_general(rows, blocks[...], contract, preferred_element_type=F32)
    part[:, nb:] = lax.dot_general(rows, finals[...], contract, preferred_element_type=F32)


def conditioning(
    times, window, labels, time_weight_in, time_weight_out, class_table, blocks, finals, steps
):
    samples = labels.shape[0]
    selector = (
        labels[:, None] == jnp.arange(class_table.shape[0], dtype=jnp.int32)[None, :]
    ).astype(BF16)
    classes = jnp.dot(selector, class_table, preferred_element_type=F32)
    columns = blocks.shape[0] + finals.shape[0]
    smem = pl.BlockSpec(memory_space=pltpu.SMEM)
    vmem = pl.BlockSpec(memory_space=pltpu.VMEM)
    return pl.pallas_call(
        functools.partial(conditioning_kernel, steps, samples),
        out_shape=[
            jax.ShapeDtypeStruct((steps * samples, columns), F32),
            jax.ShapeDtypeStruct((2 * steps, 128), F32),
        ],
        in_specs=[smem] * 3 + [vmem] * 5,
        out_specs=[vmem] * 2,
    )(
        times,
        window,
        jnp.asarray(noise_levels(TRAIN_T)),
        time_weight_in,
        time_weight_out,
        classes,
        blocks,
        finals,
    )


def ring_order(count):
    return list(range(0, count, 2)) + list(range(1, count, 2))[::-1]


ORDER = (
    "zm1", "ym0", "zp1", "yp0", "xm10/m01", "co00/m00", "cp00", "zm2", "ym1", "zp2", "yp1", "b",
    "xm20/m11", "Sm10/m01", "Xm10/m01", "zm3", "ym2", "zp3", "b", "yp2", "xm30/m21",
    "cp10/p01/p11", "Sm20/m11", "Xm20/m11", "ym3", "b", "yp3", "xm31", "Sm30/m21", "Xm30/m21",
    "cp20/p30/p21", "Sm31", "Xm31", "cp31",
)


class Mover:
    def __init__(self, groups, count):
        self.groups, self.count, self.sent, self.pin = groups, count, [], None
        self.to_core = []

    def swap(self, value, distance):
        return self._send(value, lambda i: i ^ distance, lambda g: g, distance > 1 or CORE_COUNTS)

    def across(self, value):
        return self._send(value, lambda i: i, lambda g: g ^ 1)

    def ring(self, value):
        order = ring_order(self.count // 4)
        after = {z: order[(k + 1) % len(order)] for k, z in enumerate(order)}
        return self._send(value, lambda i: after[i // 4] * 4 + i % 4, lambda g: g)

    def _send(self, value, target, side, counts=True):
        if len(self.sent) >= WINDOW:
            value, _ = lax.optimization_barrier((value, self.sent[-WINDOW]))
        if self.pin is not None:
            value, _ = lax.optimization_barrier((value, self.pin))
            self.pin = None
        pairs = [
            (g * self.count + i, side(g) * self.count + target(i))
            for g in range(self.groups)
            for i in range(self.count)
        ]
        value = lax.ppermute(value, ("group", "tm"), pairs)
        (self.sent if counts else self.to_core).append(value)
        return value


def spread_weights(first, halves, groups, count, order):
    mover = Mover(groups, count)
    side = lax.axis_index("group")
    mine = jnp.where(side == 0, halves[0], halves[1])
    other = jnp.where(side == 0, halves[1], halves[0])
    alone = {("p", 0, 0): first, ("m", 0, 0): mine, ("o", 0, 0): other}
    found, stacks = {}, {}

    def note(buffer, keys):
        row = 0
        for key in keys:
            found[key] = (buffer, row)
            row += (first if key[0] == "p" else mine).shape[0]

    def stack(keys):
        rows = [alone[key] for key in keys]
        return jnp.concatenate(rows, axis=0) if len(rows) > 1 else rows[0]

    def pieces():
        lone = [(key + (0,), rows, 0) for key, rows in alone.items()]
        return lone + [(key, *at) for key, at in found.items()]

    for op in order:
        how, kind = op[0], op[1:2]
        keys = [(k[0], int(k[1]), int(k[2])) for k in op[1:].split("/")] if how in "cxSX" else None
        if how == "z":
            r = int(op[2])
            alone[kind, r, 0] = mover.ring(alone[kind, r - 1, 0])
        elif how == "y":
            r = int(op[2])
            alone[kind, r, 1] = mover.swap(alone[kind, r, 0], 2)
        elif how == "x":
            stacks[op[1:]] = (stack(keys), mover.across(stack(keys)))
            note(stacks[op[1:]][1], [("o",) + key[1:] + (0,) for key in keys])
        elif how == "S":
            note(mover.swap(stacks[op[1:]][0], 1), [key + (1,) for key in keys])
        elif how == "X":
            note(mover.swap(stacks[op[1:]][1], 1), [("o",) + key[1:] + (1,) for key in keys])
        elif how == "c":
            note(mover.swap(stack(keys), 1), [key + (1,) for key in keys])
        elif how == "b":
            mover.pin, mover.to_core = mover.to_core, []
    return pieces()


def norm(hidden, shift, scale):
    average = jnp.mean(hidden, axis=0, keepdims=True)
    centered = hidden - average
    variance = jnp.mean(centered * centered, axis=0, keepdims=True)
    return (centered * lax.rsqrt(variance + 1e-06) * (1.0 + scale) + shift).astype(BF16)


def own_terms(packs, flat, samples):
    columns = flat.shape[1]
    position = lax.axis_index("tm")
    for ref, row, rows, shard in packs:
        pack = ref.rows(row, rows)
        where = position * samples
        pick_row = lax.broadcasted_iota(jnp.int32, (PAD, rows), 0)
        pick_of = lax.broadcasted_iota(jnp.int32, (PAD, rows), 1)
        total = jnp.zeros((PAD, columns), F32)
        for k in range(pack.shape[1] // columns):
            hit = (pick_of + k * rows == where + pick_row) & (pick_row < samples)
            pick = jnp.where(hit, 1.0, 0.0).astype(BF16)
            total = total + jnp.dot(
                pick, pack[:, k * columns : (k + 1) * columns], preferred_element_type=F32
            )
        flat[pl.ds(pl.multiple_of(shard * PAD, PAD), PAD), :] = total


def spread_terms(flat_ref, mods, nb, samples):
    columns = flat_ref.shape[1]
    sources = flat_ref.shape[0] // PAD
    tokens = mods.shape[1]
    each = tokens // samples
    block_rows = sources * nb
    flat = flat_ref[...].T.astype(BF16)
    row = lax.broadcasted_iota(jnp.int32, (sources * PAD, tokens), 0)
    sample = lax.broadcasted_iota(jnp.int32, (sources * PAD, tokens), 1) // each
    for j in range(sources):
        spans = [(j * nb, 0, nb), (block_rows + j * (columns - nb), nb, columns)]
        pick = jnp.where(row == j * PAD + sample, 1.0, 0.0).astype(BF16)
        spread = jnp.dot(flat, pick, preferred_element_type=F32)
        for d, u, v in spans:
            mods[pl.ds(d, v - u), :] = spread[u:v]


def product(places, right, limit):
    done = 0
    while done < len(places):
        batch, total = [], 0
        while done < len(places) and (not batch or total + places[done][1] <= limit):
            batch.append(places[done])
            total += places[done][1]
            done += 1
        left = [load() for load, _, _ in batch]
        left = left[0] if len(left) == 1 else jnp.concatenate(left, axis=0)
        result = jnp.dot(left, right, preferred_element_type=F32)
        start = 0
        for _, rows, place in batch:
            yield result[start : start + rows], rows, place
            start += rows


def attention_part(
    state, patch, place, term, queries, mixes, qkv, att, mixed, raised, heads, samples
):
    width, tokens = place.target.shape
    each = tokens // samples
    size = width // heads
    patches = state.ready()[...].astype(BF16)
    hidden = jnp.dot(patch.ready()[...], patches, preferred_element_type=F32)
    hidden = hidden + place.ready()[...]
    normed = norm(hidden, term(0), term(1))
    for result, rows, at in product(queries, normed, width):
        qkv[pl.ds(at, rows), :] = result.astype(BF16)
    sample_of = lax.broadcasted_iota(jnp.int32, (each, tokens), 1) // each
    scale = 1.0 / math.sqrt(size)
    for k in range(heads):
        query = qkv[pl.ds(k * size, size), :]
        key = qkv[pl.ds(width + k * size, size), :]
        scores = lax.dot_general(
            key, query, (((0,), (0,)), ((), ())), preferred_element_type=F32
        )
        mine = scores[0:each]
        for s in range(1, samples):
            mine = jnp.where(sample_of == s, scores[s * each : (s + 1) * each], mine)
        raised[pl.ds(k * each, each), :] = jnp.exp(mine * scale)
    for k in range(heads):
        value = qkv[pl.ds(2 * width + k * size, size), :]
        weights = raised[pl.ds(k * each, each), :]
        weights = weights / jnp.sum(weights, axis=0, keepdims=True)
        spread = jnp.concatenate(
            [jnp.where(sample_of == s, weights, 0.0).astype(BF16) for s in range(samples)], axis=0
        )
        att[pl.ds(k * size, size), :] = jnp.dot(
            value, spread, preferred_element_type=F32
        ).astype(BF16)
    for result, rows, at in product(mixes, att[...], width):
        mixed[pl.ds(at, rows), :] = result
    return hidden + term(2) * mixed[...]


def feed_part(hidden, state, term, out, scales, expands, shrinks, mid, mixed):
    width = hidden.shape[0]
    normed = norm(hidden, term(3), term(4))
    for result, rows, at in product(expands, normed, width):
        mid[pl.ds(at, rows), :] = jax.nn.gelu(result, approximate=True).astype(BF16)
    right = jnp.concatenate([mid[pl.ds(start, width), :] for start, _ in shrinks], axis=0)
    slices = [places for _, places in shrinks]
    joined = [
        (joined_rows([at[k][0] for at in slices]), slices[0][k][1], slices[0][k][2])
        for k in range(len(slices[0]))
    ]
    for result, rows, at in product(joined, right, width):
        mixed[pl.ds(at, rows), :] = result
    hidden = hidden + term(5) * mixed[...]
    normed = norm(hidden, term(6), term(7))
    predicted = jnp.dot(out.ready()[...], normed, preferred_element_type=F32)
    position = lax.axis_index("tm")
    scales = scales.ready()
    scale_state = scales[pl.ds(position, 1), 0:1]
    scale_noise = scales[pl.ds(scales.shape[0] // 2 + position, 1), 0:1]
    return (scale_state - 1.0) * state.ready()[...] + scale_noise * predicted


def owner(r, dy, core):
    position = lax.axis_index("tm")
    depth = lax.axis_size("tm") // 4
    z = position // 4
    spot = jnp.where(z % 2 == 0, z // 2, depth - 1 - z // 2)
    spot = (spot - r + depth) % depth
    z = jnp.where(2 * spot < depth, 2 * spot, 2 * (depth - spot) - 1)
    return z * 4 + ((position % 4) ^ (2 * dy + core))


def joined_rows(loads):
    return lambda: jnp.concatenate([one() for one in loads], axis=1)


class Fetched:
    def __init__(self, source, target, sem):
        self.target, self.copy, self.here = target, pltpu.make_async_copy(source, target, sem), False
        self.copy.start()

    def ready(self):
        if not self.here:
            self.copy.wait()
            self.here = True
        return self.target

    def rows(self, start, rows):
        return self.ready()[pl.ds(start, rows), :]


def load(ref, start, rows):
    return lambda: ref.rows(start, rows)


def placed(keys, refs, sizes):
    nq, nm, ne, ns, width, pack_rows = sizes
    queries, mixes, expands, shrinks, packs = [], [], [], [], []
    if keys[0][0] is None:
        query, mix, expand, shrink = refs
        queries.append((load(query, 0, 3 * width), 3 * width, 0))
        mixes.append((load(mix, 0, width), width, 0))
        expands = [(load(expand, k * width, width), width, k * width) for k in range(ns)]
        shrinks = [(k * width, [(load(shrink, k * width, width), width, 0)]) for k in range(ns)]
        return queries, mixes, expands, shrinks, packs
    side = lax.axis_index("group")
    he, hs = ne // 2, ns // 2
    by_slice = {(kind, k): [] for kind in "mo" for k in range(hs)}
    for (kind, r, dy, core), which, row in keys:
        ref, shard = refs[which], owner(r, dy, core)
        if kind == "p":
            queries.append((load(ref, row, nq), nq, pl.multiple_of(shard * nq, 16)))
            mixes.append((load(ref, row + nq, nm), nm, pl.multiple_of(shard * nm, 16)))
            packs.append((ref, row + nq + nm, pack_rows, shard))
            continue
        half = side if kind == "m" else 1 - side
        expands.append((load(ref, row, he), he, pl.multiple_of(shard * ne + half * he, 16)))
        for k in range(hs):
            by_slice[kind, k].append(
                (load(ref, row + he + k * nm, nm), nm, pl.multiple_of(shard * nm, 16))
            )
    for (kind, k), places in by_slice.items():
        half = side if kind == "m" else 1 - side
        shrinks.append((pl.multiple_of((half * hs + k) * width, width), places))
    return queries, mixes, expands, shrinks, packs


def network_kernel(names, keys, count, sizes, nb, heads, samples, *refs):
    width = sizes[4]
    refs = list(refs)
    take = lambda: refs.pop(0)
    given = [take() for _ in range(len(names) + count)]
    results = [take() for _ in range(2 if "terms" in names else 3)]
    fetched = [Fetched(ref, take(), refs[-1].at[k]) for k, ref in enumerate(given)]
    buffers = fetched[len(names) :]
    by_name = dict(zip(names, fetched))
    state, scales, patch, place, out, terms = (
        by_name.get(name) for name in ("state", "scales", "patch", "place", "out", "terms")
    )
    mods, mixed = take(), take()
    queries, mixes, expands, shrinks, packs = placed(keys, buffers, sizes)
    if terms is None:
        flat = results[2]
        own_terms(packs, flat, samples)
    else:
        flat = terms.ready()
    spread_terms(flat, mods, nb, samples)
    term = lambda k: mods[pl.ds(k * width, width), :]
    qkv, att, mid, raised = take(), take(), take(), take()
    hidden = attention_part(
        state, patch, place, term, queries, mixes, qkv, att, mixed, raised, heads, samples
    )
    drift = feed_part(
        hidden, state, term, out, scales, expands, shrinks, mid, mixed
    )
    results[0][...] = drift
    results[1][...] = drift.astype(BF16)
    for one in fetched:
        one.ready()


def run_network(fixed, pieces, sizes, nb, columns, heads, samples):
    width, tokens = fixed["place"].shape
    patch = fixed["state"].shape[0]
    ff = sizes[3] * width
    needs = ["terms", "state", "patch", "place", "out", "scales"]
    names = [name for name in needs if name in fixed]
    buffers, keys = [], []
    if pieces[0][0] is not None:
        pieces = sorted(pieces, key=lambda piece: (piece[0][0] != "p", piece[0][1:]))
    for key, rows, row in pieces:
        which = [k for k, known in enumerate(buffers) if known is rows]
        keys.append((key, which[0] if which else len(buffers), row))
        if not which:
            buffers.append(rows)
    operands = [fixed[name] for name in names] + buffers
    scratch = [pltpu.VMEM(rows.shape, rows.dtype) for rows in operands]
    scratch += [pltpu.VMEM((8 * width, tokens), F32), pltpu.VMEM((width, tokens), F32)]
    scratch += [
        pltpu.VMEM((3 * width, tokens), BF16),
        pltpu.VMEM((width, tokens), BF16),
        pltpu.VMEM((ff, tokens), BF16),
        pltpu.VMEM((heads * tokens // samples, tokens), F32),
    ]
    out_shape = [
        jax.ShapeDtypeStruct((patch, tokens), F32),
        jax.ShapeDtypeStruct((patch, tokens), BF16),
    ]
    if "terms" not in names:
        sources = 8 * width // columns
        out_shape.append(jax.ShapeDtypeStruct((sources * PAD, columns), F32))
    scratch.append(pltpu.SemaphoreType.DMA((len(operands),)))
    rows = 4 * width + 2 * ff
    return pl.pallas_call(
        functools.partial(
            network_kernel, names, keys, len(buffers), sizes, nb, heads, samples
        ),
        out_shape=out_shape,
        in_specs=[pl.BlockSpec(memory_space=pl.ANY)] * len(operands),
        out_specs=[pl.BlockSpec(memory_space=pltpu.VMEM)] * len(out_shape),
        scratch_shapes=scratch,
        compiler_params=pltpu.CompilerParams(vmem_limit_bytes=VMEM_LIMIT),
        cost_estimate=pl.CostEstimate(
            flops=2 * rows * width * tokens, bytes_accessed=2 * rows * width, transcendentals=0
        ),
    )(*operands)


def earlier_sum(value, narrow, count):
    position = lax.axis_index("tm")
    total = value
    before = jnp.zeros_like(value)
    distance = 1
    while distance < count:
        pairs = [(i, i ^ distance) for i in range(count)]
        other = lax.ppermute(narrow, "tm", pairs).astype(value.dtype)
        before = jnp.where((position & distance) != 0, before + other, before)
        total = total + other
        narrow = total.astype(BF16)
        distance *= 2
    return before


def body(
    noise,
    labels,
    timesteps,
    window_start,
    time_weight_in,
    time_weight_out,
    class_table,
    patch_weight,
    query_key_value,
    mix_weight,
    expand_weight,
    shrink_weight,
    block_modulation,
    final_modulation,
    output_weight,
):
    groups, count = lax.axis_size("group"), lax.axis_size("tm")
    samples, latent = noise.shape
    patch, width = patch_weight.shape
    each = latent // patch
    tokens = samples * each

    nq, nm, ne = query_key_value.shape[2], mix_weight.shape[2], expand_weight.shape[2]
    ns = shrink_weight.shape[1] // width
    columns = block_modulation.shape[2] + final_modulation.shape[1]
    packed = width // columns
    pack_rows = count * samples // max(packed, 1)
    sizes = (nq, nm, ne, ns, width, pack_rows)
    q_rows, m_rows, e_rows = query_key_value[0].T, mix_weight[0].T, expand_weight[0].T
    s_rows = shrink_weight[0].reshape(ns, width, nm).transpose(0, 2, 1)
    nb = block_modulation.shape[2]

    def prelude(times):
        return conditioning(
            times,
            window_start,
            labels,
            time_weight_in,
            time_weight_out,
            class_table,
            block_modulation[0].T,
            final_modulation.T,
            count,
        )

    place = jnp.asarray(position_columns(each, width, samples))
    part, scales = prelude(timesteps)
    start = noise.reshape(samples, each, patch).transpose(2, 0, 1).reshape(patch, tokens)
    fixed = dict(
        scales=scales, patch=patch_weight.T, place=place, out=output_weight.T, state=start
    )

    def network(pieces, **more):
        return run_network({**fixed, **more}, pieces, sizes, nb, columns, HEADS, samples)

    short = (
        groups == 2
        and count == 16
        and ns % 2 == 0
        and packed * columns == width
        and packed * pack_rows == count * samples
        and samples <= PAD
        and all(v % 16 == 0 for v in (nq, nm, ne // 2, pack_rows))
    )
    if short:
        half_e, half_s = ne // 2, ns // 2
        packs = [part[k * pack_rows : (k + 1) * pack_rows] for k in range(packed)]
        packs = jnp.concatenate(packs, axis=1).astype(BF16)
        first = jnp.concatenate([q_rows, m_rows, packs], axis=0)
        halves = [
            jnp.concatenate(
                [e_rows[k * half_e : (k + 1) * half_e]]
                + [s_rows[k * half_s + j] for j in range(half_s)],
                axis=0,
            )
            for k in range(2)
        ]
        pieces = spread_weights(first, halves, groups, count, ORDER)
        drift, narrow, terms = network(pieces)
    else:
        whole = lambda rows, axis: lax.all_gather(rows, "tm", axis=axis, tiled=True)
        terms = part.astype(BF16).reshape(count, samples, columns)
        terms = lax.all_to_all(terms, "tm", split_axis=0, concat_axis=0, tiled=True)
        terms = jnp.pad(terms.astype(F32), ((0, 0), (0, -samples % PAD), (0, 0)))
        terms = terms.reshape(count * PAD, columns)
        pieces = [
            (None, whole(q_rows, 0), 0),
            (None, whole(m_rows, 0), 0),
            (None, whole(e_rows, 0), 0),
            (None, whole(s_rows, 1).reshape(ns * width, width), 0),
        ]
        drift, narrow = network(pieces, terms=terms)

    states = start
    for sweep in range(ITERS):
        if sweep > 0:
            drift, narrow = network(pieces, terms=terms, state=states)
        before = earlier_sum(drift, narrow, count)
        running = before + drift
        states = start + before
    result = (start + running).reshape(patch, samples, each).transpose(1, 2, 0)
    return result.reshape(1, samples, latent)


def solution(mesh):
    return jax.shard_map(
        body,
        mesh=mesh,
        in_specs=(
            P("group", None),
            P("group"),
            P(),
            P(),
            P(),
            P(),
            P(),
            P(),
            P(None, None, "tm"),
            P(None, None, "tm"),
            P(None, None, "tm"),
            P(None, None, "tm"),
            P(None, None, "tm"),
            P(None, "tm"),
            P(),
        ),
        out_specs=P("tm", "group", None),
        check_vma=False,
    )
```

```python
import functools
import math

import jax
import jax.numpy as jnp
import numpy as np
from jax import lax
from jax.experimental import pallas as pl
from jax.experimental.pallas import tpu as pltpu
from jax.sharding import PartitionSpec as P

HEADS = 12
ITERS = 2
TRAIN_T = 1000
WINDOW = 5
CORE_COUNTS = False
PAD = 8
VMEM_LIMIT = 53 * 1024 * 1024
BF16 = jnp.bfloat16
F32 = jnp.float32


def noise_levels(train_steps):
    levels = np.arange(train_steps, dtype=np.float32)
    betas = np.float32(0.0001) + np.float32(0.02 - 0.0001) * levels / np.float32(train_steps - 1)
    return np.cumprod((np.float32(1.0) - betas).astype(np.float64)).astype(np.float32)


def position_columns(count, width, samples):
    side = math.isqrt(count)
    quarter = width // 4
    omega = 1.0 / 10000.0 ** (np.arange(quarter, dtype=np.float64) / quarter)
    index = np.arange(count)
    first = omega[:, None] * (index // side)[None, :]
    second = omega[:, None] * (index % side)[None, :]
    table = np.concatenate([np.sin(first), np.cos(first), np.sin(second), np.cos(second)], axis=0)
    return np.tile(table, (1, samples)).astype(np.float32)


def conditioning_kernel(
    steps, samples, times, window, levels, w_in, w_out, classes, blocks, finals, part, scales
):
    half = w_in.shape[0] // 2
    row = lax.broadcasted_iota(jnp.int32, (steps, half), 0)
    lane = lax.broadcasted_iota(jnp.int32, (steps, half), 1).astype(F32)
    place = lax.broadcasted_iota(jnp.int32, (steps, scales.shape[1]), 0)
    current = jnp.zeros((steps, half), F32)
    now = jnp.ones(place.shape, F32)
    then = jnp.ones(place.shape, F32)
    for j in range(steps):
        here, after = times[window[0] + j], times[window[0] + j + 1]
        current = jnp.where(row == j, here.astype(F32), current)
        now = jnp.where(place == j, levels[here], now)
        then = jnp.where(place == j, levels[after], then)
    scale = jnp.sqrt(then / now)
    scales[0:steps, :] = scale
    scales[steps : 2 * steps, :] = jnp.sqrt(1.0 - then) - scale * jnp.sqrt(1.0 - now)
    angles = current * jnp.exp(-math.log(10000.0) * lane / half)
    features = jnp.concatenate([jnp.cos(angles), jnp.sin(angles)], axis=1).astype(BF16)
    hidden = jax.nn.silu(jnp.dot(features, w_in[...], preferred_element_type=F32)).astype(BF16)
    embed = jnp.dot(hidden, w_out[...], preferred_element_type=F32)
    rows = jnp.concatenate(
        [jax.nn.silu(embed + classes[s : s + 1, :]).astype(BF16) for s in range(samples)], axis=0
    )
    to = lax.broadcasted_iota(jnp.int32, (rows.shape[0], rows.shape[0]), 0)
    of = lax.broadcasted_iota(jnp.int32, (rows.shape[0], rows.shape[0]), 1)
    turn = jnp.where(of == (to % samples) * steps + to // samples, 1.0, 0.0).astype(BF16)
    rows = jnp.dot(turn, rows, preferred_element_type=F32).astype(BF16)
    nb = blocks.shape[0]
    contract = (((1,), (1,)), ((), ()))
    part[:, 0:nb] = lax.dot_general(rows, blocks[...], contract, preferred_element_type=F32)
    part[:, nb:] = lax.dot_general(rows, finals[...], contract, preferred_element_type=F32)


def conditioning(
    times, window, labels, time_weight_in, time_weight_out, class_table, blocks, finals, steps
):
    samples = labels.shape[0]
    selector = (
        labels[:, None] == jnp.arange(class_table.shape[0], dtype=jnp.int32)[None, :]
    ).astype(BF16)
    classes = jnp.dot(selector, class_table, preferred_element_type=F32)
    columns = blocks.shape[0] + finals.shape[0]
    smem = pl.BlockSpec(memory_space=pltpu.SMEM)
    vmem = pl.BlockSpec(memory_space=pltpu.VMEM)
    return pl.pallas_call(
        functools.partial(conditioning_kernel, steps, samples),
        out_shape=[
            jax.ShapeDtypeStruct((steps * samples, columns), F32),
            jax.ShapeDtypeStruct((2 * steps, 128), F32),
        ],
        in_specs=[smem] * 3 + [vmem] * 5,
        out_specs=[vmem] * 2,
    )(
        times,
        window,
        jnp.asarray(noise_levels(TRAIN_T)),
        time_weight_in,
        time_weight_out,
        classes,
        blocks,
        finals,
    )


def ring_order(count):
    return list(range(0, count, 2)) + list(range(1, count, 2))[::-1]


ORDER = (
    "zm1", "ym0", "zp1", "yp0", "xm10/m01", "co00/m00", "cp00", "zm2", "ym1", "zp2", "yp1", "b",
    "xm20/m11", "Sm10/m01", "Xm10/m01", "zm3", "ym2", "zp3", "b", "yp2", "xm30/m21",
    "cp10/p01/p11", "Sm20/m11", "Xm20/m11", "ym3", "b", "yp3", "xm31", "Sm30/m21", "Xm30/m21",
    "cp20/p30/p21", "Sm31", "Xm31", "cp31",
)


class Mover:
    def __init__(self, groups, count):
        self.groups, self.count, self.sent, self.pin = groups, count, [], None
        self.to_core = []

    def swap(self, value, distance):
        return self._send(value, lambda i: i ^ distance, lambda g: g, distance > 1 or CORE_COUNTS)

    def across(self, value):
        return self._send(value, lambda i: i, lambda g: g ^ 1)

    def ring(self, value):
        order = ring_order(self.count // 4)
        after = {z: order[(k + 1) % len(order)] for k, z in enumerate(order)}
        return self._send(value, lambda i: after[i // 4] * 4 + i % 4, lambda g: g)

    def _send(self, value, target, side, counts=True):
        if len(self.sent) >= WINDOW:
            value, _ = lax.optimization_barrier((value, self.sent[-WINDOW]))
        if self.pin is not None:
            value, _ = lax.optimization_barrier((value, self.pin))
            self.pin = None
        pairs = [
            (g * self.count + i, side(g) * self.count + target(i))
            for g in range(self.groups)
            for i in range(self.count)
        ]
        value = lax.ppermute(value, ("group", "tm"), pairs)
        (self.sent if counts else self.to_core).append(value)
        return value


def spread_weights(first, halves, groups, count, order):
    mover = Mover(groups, count)
    side = lax.axis_index("group")
    mine = jnp.where(side == 0, halves[0], halves[1])
    other = jnp.where(side == 0, halves[1], halves[0])
    alone = {("p", 0, 0): first, ("m", 0, 0): mine, ("o", 0, 0): other}
    found, stacks = {}, {}

    def note(buffer, keys):
        row = 0
        for key in keys:
            found[key] = (buffer, row)
            row += (first if key[0] == "p" else mine).shape[0]

    def stack(keys):
        rows = [alone[key] for key in keys]
        return jnp.concatenate(rows, axis=0) if len(rows) > 1 else rows[0]

    def pieces():
        lone = [(key + (0,), rows, 0) for key, rows in alone.items()]
        return lone + [(key, *at) for key, at in found.items()]

    for op in order:
        how, kind = op[0], op[1:2]
        keys = [(k[0], int(k[1]), int(k[2])) for k in op[1:].split("/")] if how in "cxSX" else None
        if how == "z":
            r = int(op[2])
            alone[kind, r, 0] = mover.ring(alone[kind, r - 1, 0])
        elif how == "y":
            r = int(op[2])
            alone[kind, r, 1] = mover.swap(alone[kind, r, 0], 2)
        elif how == "x":
            stacks[op[1:]] = (stack(keys), mover.across(stack(keys)))
            note(stacks[op[1:]][1], [("o",) + key[1:] + (0,) for key in keys])
        elif how == "S":
            note(mover.swap(stacks[op[1:]][0], 1), [key + (1,) for key in keys])
        elif how == "X":
            note(mover.swap(stacks[op[1:]][1], 1), [("o",) + key[1:] + (1,) for key in keys])
        elif how == "c":
            note(mover.swap(stack(keys), 1), [key + (1,) for key in keys])
        elif how == "b":
            mover.pin, mover.to_core = mover.to_core, []
    return pieces()


def norm(hidden, shift, scale):
    average = jnp.mean(hidden, axis=0, keepdims=True)
    centered = hidden - average
    variance = jnp.mean(centered * centered, axis=0, keepdims=True)
    return (centered * lax.rsqrt(variance + 1e-06) * (1.0 + scale) + shift).astype(BF16)


def own_terms(packs, flat, samples):
    columns = flat.shape[1]
    position = lax.axis_index("tm")
    for ref, row, rows, shard in packs:
        pack = ref.rows(row, rows)
        where = position * samples
        pick_row = lax.broadcasted_iota(jnp.int32, (PAD, rows), 0)
        pick_of = lax.broadcasted_iota(jnp.int32, (PAD, rows), 1)
        total = jnp.zeros((PAD, columns), F32)
        for k in range(pack.shape[1] // columns):
            hit = (pick_of + k * rows == where + pick_row) & (pick_row < samples)
            pick = jnp.where(hit, 1.0, 0.0).astype(BF16)
            total = total + jnp.dot(
                pick, pack[:, k * columns : (k + 1) * columns], preferred_element_type=F32
            )
        flat[pl.ds(pl.multiple_of(shard * PAD, PAD), PAD), :] = total


def spread_terms(flat_ref, mods, nb, samples):
    columns = flat_ref.shape[1]
    sources = flat_ref.shape[0] // PAD
    tokens = mods.shape[1]
    each = tokens // samples
    block_rows = sources * nb
    flat = flat_ref[...].T.astype(BF16)
    row = lax.broadcasted_iota(jnp.int32, (sources * PAD, tokens), 0)
    sample = lax.broadcasted_iota(jnp.int32, (sources * PAD, tokens), 1) // each
    for j in range(sources):
        spans = [(j * nb, 0, nb), (block_rows + j * (columns - nb), nb, columns)]
        pick = jnp.where(row == j * PAD + sample, 1.0, 0.0).astype(BF16)
        spread = jnp.dot(flat, pick, preferred_element_type=F32)
        for d, u, v in spans:
            mods[pl.ds(d, v - u), :] = spread[u:v]


def product(places, right, limit):
    done = 0
    while done < len(places):
        batch, total = [], 0
        while done < len(places) and (not batch or total + places[done][1] <= limit):
            batch.append(places[done])
            total += places[done][1]
            done += 1
        left = [load() for load, _, _ in batch]
        left = left[0] if len(left) == 1 else jnp.concatenate(left, axis=0)
        result = jnp.dot(left, right, preferred_element_type=F32)
        start = 0
        for _, rows, place in batch:
            yield result[start : start + rows], rows, place
            start += rows


def attention_part(
    state, patch, place, term, queries, mixes, qkv, att, mixed, raised, heads, samples, landed
):
    width, tokens = place.target.shape
    each = tokens // samples
    size = width // heads
    patches = state.ready()[...].astype(BF16)
    hidden = jnp.dot(patch.ready()[...], patches, preferred_element_type=F32)
    hidden = hidden + place.ready()[...]
    normed = norm(hidden, term(0), term(1))
    landed()
    for result, rows, at in product(queries, normed, width):
        qkv[pl.ds(at, rows), :] = result.astype(BF16)
    sample_of = lax.broadcasted_iota(jnp.int32, (each, tokens), 1) // each
    scale = 1.0 / math.sqrt(size)
    for k in range(heads):
        query = qkv[pl.ds(k * size, size), :]
        key = qkv[pl.ds(width + k * size, size), :]
        scores = lax.dot_general(
            key, query, (((0,), (0,)), ((), ())), preferred_element_type=F32
        )
        mine = scores[0:each]
        for s in range(1, samples):
            mine = jnp.where(sample_of == s, scores[s * each : (s + 1) * each], mine)
        raised[pl.ds(k * each, each), :] = jnp.exp(mine * scale)
    for k in range(heads):
        value = qkv[pl.ds(2 * width + k * size, size), :]
        weights = raised[pl.ds(k * each, each), :]
        weights = weights / jnp.sum(weights, axis=0, keepdims=True)
        spread = jnp.concatenate(
            [jnp.where(sample_of == s, weights, 0.0).astype(BF16) for s in range(samples)], axis=0
        )
        att[pl.ds(k * size, size), :] = jnp.dot(
            value, spread, preferred_element_type=F32
        ).astype(BF16)
    for result, rows, at in product(mixes, att[...], width):
        mixed[pl.ds(at, rows), :] = result
    return hidden + term(2) * mixed[...]


def feed_part(hidden, state, term, out, scales, expands, shrinks, mid, mixed):
    width = hidden.shape[0]
    normed = norm(hidden, term(3), term(4))
    for result, rows, at in product(expands, normed, width):
        mid[pl.ds(at, rows), :] = jax.nn.gelu(result, approximate=True).astype(BF16)
    right = jnp.concatenate([mid[pl.ds(start, width), :] for start, _ in shrinks], axis=0)
    slices = [places for _, places in shrinks]
    joined = [
        (joined_rows([at[k][0] for at in slices]), slices[0][k][1], slices[0][k][2])
        for k in range(len(slices[0]))
    ]
    for result, rows, at in product(joined, right, width):
        mixed[pl.ds(at, rows), :] = result
    hidden = hidden + term(5) * mixed[...]
    normed = norm(hidden, term(6), term(7))
    predicted = jnp.dot(out.ready()[...], normed, preferred_element_type=F32)
    position = lax.axis_index("tm")
    scales = scales.ready()
    scale_state = scales[pl.ds(position, 1), 0:1]
    scale_noise = scales[pl.ds(scales.shape[0] // 2 + position, 1), 0:1]
    return (scale_state - 1.0) * state.ready()[...] + scale_noise * predicted


def owner(r, dy, core):
    position = lax.axis_index("tm")
    depth = lax.axis_size("tm") // 4
    z = position // 4
    spot = jnp.where(z % 2 == 0, z // 2, depth - 1 - z // 2)
    spot = (spot - r + depth) % depth
    z = jnp.where(2 * spot < depth, 2 * spot, 2 * (depth - spot) - 1)
    return z * 4 + ((position % 4) ^ (2 * dy + core))


def joined_rows(loads):
    return lambda: jnp.concatenate([one() for one in loads], axis=1)


class Fetched:
    def __init__(self, source, target, sem):
        self.target, self.copy, self.here = target, pltpu.make_async_copy(source, target, sem), False

    def begin(self):
        self.copy.start()

    def ready(self):
        if not self.here:
            self.copy.wait()
            self.here = True
        return self.target

    def rows(self, start, rows):
        return self.ready()[pl.ds(start, rows), :]


def load(ref, start, rows):
    return lambda: ref.rows(start, rows)


def placed(keys, refs, sizes):
    nq, nm, ne, ns, width, pack_rows = sizes
    queries, mixes, expands, shrinks, packs = [], [], [], [], []
    if keys[0][0] is None:
        query, mix, expand, shrink = refs
        queries.append((load(query, 0, 3 * width), 3 * width, 0))
        mixes.append((load(mix, 0, width), width, 0))
        expands = [(load(expand, k * width, width), width, k * width) for k in range(ns)]
        shrinks = [(k * width, [(load(shrink, k * width, width), width, 0)]) for k in range(ns)]
        return queries, mixes, expands, shrinks, packs
    side = lax.axis_index("group")
    he, hs = ne // 2, ns // 2
    by_slice = {(kind, k): [] for kind in "mo" for k in range(hs)}
    for (kind, r, dy, core), which, row in keys:
        ref, shard = refs[which], owner(r, dy, core)
        if kind == "p":
            queries.append((load(ref, row, nq), nq, pl.multiple_of(shard * nq, 16)))
            mixes.append((load(ref, row + nq, nm), nm, pl.multiple_of(shard * nm, 16)))
            packs.append((ref, row + nq + nm, pack_rows, shard))
            continue
        half = side if kind == "m" else 1 - side
        expands.append((load(ref, row, he), he, pl.multiple_of(shard * ne + half * he, 16)))
        for k in range(hs):
            by_slice[kind, k].append(
                (load(ref, row + he + k * nm, nm), nm, pl.multiple_of(shard * nm, 16))
            )
    for (kind, k), places in by_slice.items():
        half = side if kind == "m" else 1 - side
        shrinks.append((pl.multiple_of((half * hs + k) * width, width), places))
    return queries, mixes, expands, shrinks, packs


def network_kernel(names, keys, count, sizes, nb, heads, samples, *refs):
    width = sizes[4]
    refs = list(refs)
    take = lambda: refs.pop(0)
    given = [take() for _ in range(len(names) + count)]
    results = [take() for _ in range(2 if "terms" in names else 3)]
    fetched = [Fetched(ref, take(), refs[-1].at[k]) for k, ref in enumerate(given)]
    buffers = fetched[len(names) :]
    early = {0, 1} if keys[0][0] is None else {which for key, which, _ in keys if key[0] == "p"}
    soon = [one for k, one in enumerate(buffers) if k in early]
    later = [one for k, one in enumerate(buffers) if k not in early]
    for one in fetched[: len(names)] + soon:
        one.begin()

    def landed():
        for one in soon:
            one.ready()
        for one in later:
            one.begin()

    by_name = dict(zip(names, fetched))
    state, scales, patch, place, out, terms = (
        by_name.get(name) for name in ("state", "scales", "patch", "place", "out", "terms")
    )
    mods, mixed = take(), take()
    queries, mixes, expands, shrinks, packs = placed(keys, buffers, sizes)
    if terms is None:
        flat = results[2]
        own_terms(packs, flat, samples)
    else:
        flat = terms.ready()
    spread_terms(flat, mods, nb, samples)
    term = lambda k: mods[pl.ds(k * width, width), :]
    qkv, att, mid, raised = take(), take(), take(), take()
    hidden = attention_part(
        state, patch, place, term, queries, mixes, qkv, att, mixed, raised, heads, samples, landed
    )
    drift = feed_part(
        hidden, state, term, out, scales, expands, shrinks, mid, mixed
    )
    results[0][...] = drift
    results[1][...] = drift.astype(BF16)
    for one in fetched:
        one.ready()


def run_network(fixed, pieces, sizes, nb, columns, heads, samples):
    width, tokens = fixed["place"].shape
    patch = fixed["state"].shape[0]
    ff = sizes[3] * width
    needs = ["terms", "state", "patch", "place", "out", "scales"]
    names = [name for name in needs if name in fixed]
    buffers, keys = [], []
    if pieces[0][0] is not None:
        pieces = sorted(pieces, key=lambda piece: (piece[0][0] != "p", piece[0][1:]))
    for key, rows, row in pieces:
        which = [k for k, known in enumerate(buffers) if known is rows]
        keys.append((key, which[0] if which else len(buffers), row))
        if not which:
            buffers.append(rows)
    operands = [fixed[name] for name in names] + buffers
    scratch = [pltpu.VMEM(rows.shape, rows.dtype) for rows in operands]
    scratch += [pltpu.VMEM((8 * width, tokens), F32), pltpu.VMEM((width, tokens), F32)]
    scratch += [
        pltpu.VMEM((3 * width, tokens), BF16),
        pltpu.VMEM((width, tokens), BF16),
        pltpu.VMEM((ff, tokens), BF16),
        pltpu.VMEM((heads * tokens // samples, tokens), F32),
    ]
    out_shape = [
        jax.ShapeDtypeStruct((patch, tokens), F32),
        jax.ShapeDtypeStruct((patch, tokens), BF16),
    ]
    if "terms" not in names:
        sources = 8 * width // columns
        out_shape.append(jax.ShapeDtypeStruct((sources * PAD, columns), F32))
    scratch.append(pltpu.SemaphoreType.DMA((len(operands),)))
    rows = 4 * width + 2 * ff
    return pl.pallas_call(
        functools.partial(
            network_kernel, names, keys, len(buffers), sizes, nb, heads, samples
        ),
        out_shape=out_shape,
        in_specs=[pl.BlockSpec(memory_space=pl.ANY)] * len(operands),
        out_specs=[pl.BlockSpec(memory_space=pltpu.VMEM)] * len(out_shape),
        scratch_shapes=scratch,
        compiler_params=pltpu.CompilerParams(vmem_limit_bytes=VMEM_LIMIT),
        cost_estimate=pl.CostEstimate(
            flops=2 * rows * width * tokens, bytes_accessed=2 * rows * width, transcendentals=0
        ),
    )(*operands)


def earlier_sum(value, narrow, count):
    position = lax.axis_index("tm")
    total = value
    before = jnp.zeros_like(value)
    low = 1
    while low < count:
        wide = low in (1, 4) and low * 2 < count
        distances = (low, 2 * low, 3 * low) if wide else (low,)
        others = [
            lax.ppermute(narrow, "tm", [(i, i ^ far) for i in range(count)]) for far in distances
        ]
        for far, other in zip(distances, others):
            other = other.astype(value.dtype)
            top = 2 * low if far > low else low
            before = jnp.where((position & top) != 0, before + other, before)
            total = total + other
        narrow = total.astype(BF16)
        low *= 4 if wide else 2
    return before


def body(
    noise,
    labels,
    timesteps,
    window_start,
    time_weight_in,
    time_weight_out,
    class_table,
    patch_weight,
    query_key_value,
    mix_weight,
    expand_weight,
    shrink_weight,
    block_modulation,
    final_modulation,
    output_weight,
):
    groups, count = lax.axis_size("group"), lax.axis_size("tm")
    samples, latent = noise.shape
    patch, width = patch_weight.shape
    each = latent // patch
    tokens = samples * each

    nq, nm, ne = query_key_value.shape[2], mix_weight.shape[2], expand_weight.shape[2]
    ns = shrink_weight.shape[1] // width
    columns = block_modulation.shape[2] + final_modulation.shape[1]
    packed = width // columns
    pack_rows = count * samples // max(packed, 1)
    sizes = (nq, nm, ne, ns, width, pack_rows)
    q_rows, m_rows, e_rows = query_key_value[0].T, mix_weight[0].T, expand_weight[0].T
    s_rows = shrink_weight[0].reshape(ns, width, nm).transpose(0, 2, 1)
    nb = block_modulation.shape[2]

    def prelude(times):
        return conditioning(
            times,
            window_start,
            labels,
            time_weight_in,
            time_weight_out,
            class_table,
            block_modulation[0].T,
            final_modulation.T,
            count,
        )

    place = jnp.asarray(position_columns(each, width, samples))
    part, scales = prelude(timesteps)
    start = noise.reshape(samples, each, patch).transpose(2, 0, 1).reshape(patch, tokens)
    fixed = dict(
        scales=scales, patch=patch_weight.T, place=place, out=output_weight.T, state=start
    )

    def network(pieces, **more):
        return run_network({**fixed, **more}, pieces, sizes, nb, columns, HEADS, samples)

    short = (
        groups == 2
        and count == 16
        and ns % 2 == 0
        and packed * columns == width
        and packed * pack_rows == count * samples
        and samples <= PAD
        and all(v % 16 == 0 for v in (nq, nm, ne // 2, pack_rows))
    )
    if short:
        half_e, half_s = ne // 2, ns // 2
        packs = [part[k * pack_rows : (k + 1) * pack_rows] for k in range(packed)]
        packs = jnp.concatenate(packs, axis=1).astype(BF16)
        first = jnp.concatenate([q_rows, m_rows, packs], axis=0)
        halves = [
            jnp.concatenate(
                [e_rows[k * half_e : (k + 1) * half_e]]
                + [s_rows[k * half_s + j] for j in range(half_s)],
                axis=0,
            )
            for k in range(2)
        ]
        pieces = spread_weights(first, halves, groups, count, ORDER)
        drift, narrow, terms = network(pieces)
    else:
        whole = lambda rows, axis: lax.all_gather(rows, "tm", axis=axis, tiled=True)
        terms = part.astype(BF16).reshape(count, samples, columns)
        terms = lax.all_to_all(terms, "tm", split_axis=0, concat_axis=0, tiled=True)
        terms = jnp.pad(terms.astype(F32), ((0, 0), (0, -samples % PAD), (0, 0)))
        terms = terms.reshape(count * PAD, columns)
        pieces = [
            (None, whole(q_rows, 0), 0),
            (None, whole(m_rows, 0), 0),
            (None, whole(e_rows, 0), 0),
            (None, whole(s_rows, 1).reshape(ns * width, width), 0),
        ]
        drift, narrow = network(pieces, terms=terms)

    states = start
    for sweep in range(ITERS):
        if sweep > 0:
            drift, narrow = network(pieces, terms=terms, state=states)
        before = earlier_sum(drift, narrow, count)
        running = before + drift
        states = start + before
    result = (start + running).reshape(patch, samples, each).transpose(1, 2, 0)
    return result.reshape(1, samples, latent)


def solution(mesh):
    return jax.shard_map(
        body,
        mesh=mesh,
        in_specs=(
            P("group", None),
            P("group"),
            P(),
            P(),
            P(),
            P(),
            P(),
            P(),
            P(None, None, "tm"),
            P(None, None, "tm"),
            P(None, None, "tm"),
            P(None, None, "tm"),
            P(None, None, "tm"),
            P(None, "tm"),
            P(),
        ),
        out_specs=P("tm", "group", None),
        check_vma=False,
    )
```

```python
import functools
import math

import jax
import jax.numpy as jnp
import numpy as np
from jax import lax
from jax.experimental import pallas as pl
from jax.experimental.pallas import tpu as pltpu
from jax.sharding import PartitionSpec as P

HEADS = 12
ITERS = 2
TRAIN_T = 1000
WINDOW = 5
CORE_COUNTS = False
PAD = 8
VMEM_LIMIT = 53 * 1024 * 1024
BF16 = jnp.bfloat16
F32 = jnp.float32


def noise_levels(train_steps):
    levels = np.arange(train_steps, dtype=np.float32)
    betas = np.float32(0.0001) + np.float32(0.02 - 0.0001) * levels / np.float32(train_steps - 1)
    return np.cumprod((np.float32(1.0) - betas).astype(np.float64)).astype(np.float32)


def position_columns(count, width, samples):
    side = math.isqrt(count)
    quarter = width // 4
    omega = 1.0 / 10000.0 ** (np.arange(quarter, dtype=np.float64) / quarter)
    index = np.arange(count)
    first = omega[:, None] * (index // side)[None, :]
    second = omega[:, None] * (index % side)[None, :]
    table = np.concatenate([np.sin(first), np.cos(first), np.sin(second), np.cos(second)], axis=0)
    return np.tile(table, (1, samples)).astype(np.float32)


def conditioning_kernel(
    steps, samples, times, window, levels, w_in, w_out, classes, blocks, finals, part, scales
):
    half = w_in.shape[0] // 2
    row = lax.broadcasted_iota(jnp.int32, (steps, half), 0)
    lane = lax.broadcasted_iota(jnp.int32, (steps, half), 1).astype(F32)
    place = lax.broadcasted_iota(jnp.int32, (steps, scales.shape[1]), 0)
    current = jnp.zeros((steps, half), F32)
    now = jnp.ones(place.shape, F32)
    then = jnp.ones(place.shape, F32)
    for j in range(steps):
        here, after = times[window[0] + j], times[window[0] + j + 1]
        current = jnp.where(row == j, here.astype(F32), current)
        now = jnp.where(place == j, levels[here], now)
        then = jnp.where(place == j, levels[after], then)
    scale = jnp.sqrt(then / now)
    scales[0:steps, :] = scale
    scales[steps : 2 * steps, :] = jnp.sqrt(1.0 - then) - scale * jnp.sqrt(1.0 - now)
    angles = current * jnp.exp(-math.log(10000.0) * lane / half)
    features = jnp.concatenate([jnp.cos(angles), jnp.sin(angles)], axis=1).astype(BF16)
    hidden = jax.nn.silu(jnp.dot(features, w_in[...], preferred_element_type=F32)).astype(BF16)
    embed = jnp.dot(hidden, w_out[...], preferred_element_type=F32)
    rows = jnp.concatenate(
        [jax.nn.silu(embed + classes[s : s + 1, :]).astype(BF16) for s in range(samples)], axis=0
    )
    to = lax.broadcasted_iota(jnp.int32, (rows.shape[0], rows.shape[0]), 0)
    of = lax.broadcasted_iota(jnp.int32, (rows.shape[0], rows.shape[0]), 1)
    turn = jnp.where(of == (to % samples) * steps + to // samples, 1.0, 0.0).astype(BF16)
    rows = jnp.dot(turn, rows, preferred_element_type=F32).astype(BF16)
    nb = blocks.shape[0]
    contract = (((1,), (1,)), ((), ()))
    part[:, 0:nb] = lax.dot_general(rows, blocks[...], contract, preferred_element_type=F32)
    part[:, nb:] = lax.dot_general(rows, finals[...], contract, preferred_element_type=F32)


def conditioning(
    times, window, labels, time_weight_in, time_weight_out, class_table, blocks, finals, steps
):
    samples = labels.shape[0]
    selector = (
        labels[:, None] == jnp.arange(class_table.shape[0], dtype=jnp.int32)[None, :]
    ).astype(BF16)
    classes = jnp.dot(selector, class_table, preferred_element_type=F32)
    columns = blocks.shape[0] + finals.shape[0]
    smem = pl.BlockSpec(memory_space=pltpu.SMEM)
    vmem = pl.BlockSpec(memory_space=pltpu.VMEM)
    return pl.pallas_call(
        functools.partial(conditioning_kernel, steps, samples),
        out_shape=[
            jax.ShapeDtypeStruct((steps * samples, columns), F32),
            jax.ShapeDtypeStruct((2 * steps, 128), F32),
        ],
        in_specs=[smem] * 3 + [vmem] * 5,
        out_specs=[vmem] * 2,
    )(
        times,
        window,
        jnp.asarray(noise_levels(TRAIN_T)),
        time_weight_in,
        time_weight_out,
        classes,
        blocks,
        finals,
    )


def ring_order(count):
    return list(range(0, count, 2)) + list(range(1, count, 2))[::-1]


ORDER = (
    "zm1", "ym0", "zp1", "yp0", "xm10/m01", "co00/m00", "cp00", "zm2", "ym1", "zp2", "yp1", "b",
    "xm20/m11", "Sm10/m01", "Xm10/m01", "zm3", "ym2", "zp3", "b", "yp2", "xm30/m21",
    "cp10/p01/p11", "Sm20/m11", "Xm20/m11", "ym3", "b", "yp3", "xm31", "Sm30/m21", "Xm30/m21",
    "cp20/p30/p21", "Sm31", "Xm31", "cp31",
)


class Mover:
    def __init__(self, groups, count):
        self.groups, self.count, self.sent, self.pin = groups, count, [], None
        self.to_core = []

    def swap(self, value, distance):
        return self._send(value, lambda i: i ^ distance, lambda g: g, distance > 1 or CORE_COUNTS)

    def across(self, value):
        return self._send(value, lambda i: i, lambda g: g ^ 1)

    def ring(self, value):
        order = ring_order(self.count // 4)
        after = {z: order[(k + 1) % len(order)] for k, z in enumerate(order)}
        return self._send(value, lambda i: after[i // 4] * 4 + i % 4, lambda g: g)

    def _send(self, value, target, side, counts=True):
        if len(self.sent) >= WINDOW:
            value, _ = lax.optimization_barrier((value, self.sent[-WINDOW]))
        if self.pin is not None:
            value, _ = lax.optimization_barrier((value, self.pin))
            self.pin = None
        pairs = [
            (g * self.count + i, side(g) * self.count + target(i))
            for g in range(self.groups)
            for i in range(self.count)
        ]
        value = lax.ppermute(value, ("group", "tm"), pairs)
        (self.sent if counts else self.to_core).append(value)
        return value


def spread_weights(first, halves, groups, count, order):
    mover = Mover(groups, count)
    side = lax.axis_index("group")
    mine = jnp.where(side == 0, halves[0], halves[1])
    other = jnp.where(side == 0, halves[1], halves[0])
    alone = {("p", 0, 0): first, ("m", 0, 0): mine, ("o", 0, 0): other}
    found, stacks = {}, {}

    def note(buffer, keys):
        row = 0
        for key in keys:
            found[key] = (buffer, row)
            row += (first if key[0] == "p" else mine).shape[0]

    def stack(keys):
        rows = [alone[key] for key in keys]
        return jnp.concatenate(rows, axis=0) if len(rows) > 1 else rows[0]

    def pieces():
        lone = [(key + (0,), rows, 0) for key, rows in alone.items()]
        return lone + [(key, *at) for key, at in found.items()]

    for op in order:
        how, kind = op[0], op[1:2]
        keys = [(k[0], int(k[1]), int(k[2])) for k in op[1:].split("/")] if how in "cxSX" else None
        if how == "z":
            r = int(op[2])
            alone[kind, r, 0] = mover.ring(alone[kind, r - 1, 0])
        elif how == "y":
            r = int(op[2])
            alone[kind, r, 1] = mover.swap(alone[kind, r, 0], 2)
        elif how == "x":
            stacks[op[1:]] = (stack(keys), mover.across(stack(keys)))
            note(stacks[op[1:]][1], [("o",) + key[1:] + (0,) for key in keys])
        elif how == "S":
            note(mover.swap(stacks[op[1:]][0], 1), [key + (1,) for key in keys])
        elif how == "X":
            note(mover.swap(stacks[op[1:]][1], 1), [("o",) + key[1:] + (1,) for key in keys])
        elif how == "c":
            note(mover.swap(stack(keys), 1), [key + (1,) for key in keys])
        elif how == "b":
            mover.pin, mover.to_core = mover.to_core, []
    return pieces()


def norm(hidden, shift, scale):
    average = jnp.mean(hidden, axis=0, keepdims=True)
    centered = hidden - average
    variance = jnp.mean(centered * centered, axis=0, keepdims=True)
    return (centered * lax.rsqrt(variance + 1e-06) * (1.0 + scale) + shift).astype(BF16)


def own_terms(packs, flat, samples):
    columns = flat.shape[1]
    position = lax.axis_index("tm")
    for ref, row, rows, shard in packs:
        pack = ref.rows(row, rows)
        where = position * samples
        pick_row = lax.broadcasted_iota(jnp.int32, (PAD, rows), 0)
        pick_of = lax.broadcasted_iota(jnp.int32, (PAD, rows), 1)
        total = jnp.zeros((PAD, columns), F32)
        for k in range(pack.shape[1] // columns):
            hit = (pick_of + k * rows == where + pick_row) & (pick_row < samples)
            pick = jnp.where(hit, 1.0, 0.0).astype(BF16)
            total = total + jnp.dot(
                pick, pack[:, k * columns : (k + 1) * columns], preferred_element_type=F32
            )
        flat[pl.ds(pl.multiple_of(shard * PAD, PAD), PAD), :] = total


def spread_terms(flat_ref, mods, nb, samples):
    columns = flat_ref.shape[1]
    sources = flat_ref.shape[0] // PAD
    tokens = mods.shape[1]
    each = tokens // samples
    block_rows = sources * nb
    flat = flat_ref[...].T.astype(BF16)
    row = lax.broadcasted_iota(jnp.int32, (sources * PAD, tokens), 0)
    sample = lax.broadcasted_iota(jnp.int32, (sources * PAD, tokens), 1) // each
    for j in range(sources):
        spans = [(j * nb, 0, nb), (block_rows + j * (columns - nb), nb, columns)]
        pick = jnp.where(row == j * PAD + sample, 1.0, 0.0).astype(BF16)
        spread = jnp.dot(flat, pick, preferred_element_type=F32)
        for d, u, v in spans:
            mods[pl.ds(d, v - u), :] = spread[u:v]


def product(places, right, limit):
    done = 0
    while done < len(places):
        batch, total = [], 0
        while done < len(places) and (not batch or total + places[done][1] <= limit):
            batch.append(places[done])
            total += places[done][1]
            done += 1
        left = [load() for load, _, _ in batch]
        left = left[0] if len(left) == 1 else jnp.concatenate(left, axis=0)
        result = jnp.dot(left, right, preferred_element_type=F32)
        start = 0
        for _, rows, place in batch:
            yield result[start : start + rows], rows, place
            start += rows


def attention_part(
    state, patch, place, term, queries, mixes, qkv, att, mixed, raised, heads, samples, landed
):
    width, tokens = place.target.shape
    each = tokens // samples
    size = width // heads
    patches = state.ready()[...].astype(BF16)
    hidden = jnp.dot(patch.ready()[...], patches, preferred_element_type=F32)
    hidden = hidden + place.ready()[...]
    normed = norm(hidden, term(0), term(1))
    landed()
    for result, rows, at in product(queries, normed, width):
        qkv[pl.ds(at, rows), :] = result.astype(BF16)
    sample_of = lax.broadcasted_iota(jnp.int32, (each, tokens), 1) // each
    scale = 1.0 / math.sqrt(size)
    for k in range(heads):
        query = qkv[pl.ds(k * size, size), :]
        key = qkv[pl.ds(width + k * size, size), :]
        scores = lax.dot_general(
            key, query, (((0,), (0,)), ((), ())), preferred_element_type=F32
        )
        mine = scores[0:each]
        for s in range(1, samples):
            mine = jnp.where(sample_of == s, scores[s * each : (s + 1) * each], mine)
        raised[pl.ds(k * each, each), :] = jnp.exp(mine * scale)
    for k in range(heads):
        value = qkv[pl.ds(2 * width + k * size, size), :]
        weights = raised[pl.ds(k * each, each), :]
        weights = weights / jnp.sum(weights, axis=0, keepdims=True)
        spread = jnp.concatenate(
            [jnp.where(sample_of == s, weights, 0.0).astype(BF16) for s in range(samples)], axis=0
        )
        att[pl.ds(k * size, size), :] = jnp.dot(
            value, spread, preferred_element_type=F32
        ).astype(BF16)
    for result, rows, at in product(mixes, att[...], width):
        mixed[pl.ds(at, rows), :] = result
    return hidden + term(2) * mixed[...]


def feed_part(hidden, state, term, out, scales, expands, shrinks, mid, mixed):
    width = hidden.shape[0]
    normed = norm(hidden, term(3), term(4))
    for result, rows, at in product(expands, normed, width):
        mid[pl.ds(at, rows), :] = jax.nn.gelu(result, approximate=True).astype(BF16)
    right = jnp.concatenate([mid[pl.ds(start, width), :] for start, _ in shrinks], axis=0)
    slices = [places for _, places in shrinks]
    joined = [
        (joined_rows([at[k][0] for at in slices]), slices[0][k][1], slices[0][k][2])
        for k in range(len(slices[0]))
    ]
    for result, rows, at in product(joined, right, width):
        mixed[pl.ds(at, rows), :] = result
    hidden = hidden + term(5) * mixed[...]
    normed = norm(hidden, term(6), term(7))
    predicted = jnp.dot(out.ready()[...], normed, preferred_element_type=F32)
    position = lax.axis_index("tm")
    scales = scales.ready()
    scale_state = scales[pl.ds(position, 1), 0:1]
    scale_noise = scales[pl.ds(scales.shape[0] // 2 + position, 1), 0:1]
    return (scale_state - 1.0) * state.ready()[...] + scale_noise * predicted


def owner(r, dy, core):
    position = lax.axis_index("tm")
    depth = lax.axis_size("tm") // 4
    z = position // 4
    spot = jnp.where(z % 2 == 0, z // 2, depth - 1 - z // 2)
    spot = (spot - r + depth) % depth
    z = jnp.where(2 * spot < depth, 2 * spot, 2 * (depth - spot) - 1)
    return z * 4 + ((position % 4) ^ (2 * dy + core))


def joined_rows(loads):
    return lambda: jnp.concatenate([one() for one in loads], axis=1)


class Fetched:
    def __init__(self, source, target, sem):
        self.target, self.copy, self.here = target, pltpu.make_async_copy(source, target, sem), False

    def begin(self):
        self.copy.start()

    def ready(self):
        if not self.here:
            self.copy.wait()
            self.here = True
        return self.target

    def rows(self, start, rows):
        return self.ready()[pl.ds(start, rows), :]


def load(ref, start, rows):
    return lambda: ref.rows(start, rows)


def placed(keys, refs, sizes):
    nq, nm, ne, ns, width, pack_rows = sizes
    queries, mixes, expands, shrinks, packs = [], [], [], [], []
    if keys[0][0] is None:
        query, mix, expand, shrink = refs
        queries.append((load(query, 0, 3 * width), 3 * width, 0))
        mixes.append((load(mix, 0, width), width, 0))
        expands = [(load(expand, k * width, width), width, k * width) for k in range(ns)]
        shrinks = [(k * width, [(load(shrink, k * width, width), width, 0)]) for k in range(ns)]
        return queries, mixes, expands, shrinks, packs
    side = lax.axis_index("group")
    he, hs = ne // 2, ns // 2
    by_slice = {(kind, k): [] for kind in "mo" for k in range(hs)}
    for (kind, r, dy, core), which, row in keys:
        ref, shard = refs[which], owner(r, dy, core)
        if kind == "p":
            queries.append((load(ref, row, nq), nq, pl.multiple_of(shard * nq, 16)))
            mixes.append((load(ref, row + nq, nm), nm, pl.multiple_of(shard * nm, 16)))
            packs.append((ref, row + nq + nm, pack_rows, shard))
            continue
        half = side if kind == "m" else 1 - side
        expands.append((load(ref, row, he), he, pl.multiple_of(shard * ne + half * he, 16)))
        for k in range(hs):
            by_slice[kind, k].append(
                (load(ref, row + he + k * nm, nm), nm, pl.multiple_of(shard * nm, 16))
            )
    for (kind, k), places in by_slice.items():
        half = side if kind == "m" else 1 - side
        shrinks.append((pl.multiple_of((half * hs + k) * width, width), places))
    return queries, mixes, expands, shrinks, packs


def network_kernel(names, keys, count, sizes, nb, heads, samples, *refs):
    width = sizes[4]
    refs = list(refs)
    take = lambda: refs.pop(0)
    given = [take() for _ in range(len(names) + count)]
    results = [take() for _ in range(2 if "terms" in names else 3)]
    fetched = [Fetched(ref, take(), refs[-1].at[k]) for k, ref in enumerate(given)]
    buffers = fetched[len(names) :]
    early = {0, 1} if keys[0][0] is None else {which for key, which, _ in keys if key[0] == "p"}
    soon = [one for k, one in enumerate(buffers) if k in early]
    later = [one for k, one in enumerate(buffers) if k not in early]
    for one in fetched[: len(names)] + soon:
        one.begin()

    def landed():
        for one in soon:
            one.ready()
        while later:
            later.pop(0).begin()

    by_name = dict(zip(names, fetched))
    state, scales, patch, place, out, terms = (
        by_name.get(name) for name in ("state", "scales", "patch", "place", "out", "terms")
    )
    mods, mixed = take(), take()
    queries, mixes, expands, shrinks, packs = placed(keys, buffers, sizes)
    if terms is None:
        flat = results[2]
        own_terms(packs, flat, samples)
        landed()
    else:
        flat = terms.ready()
    spread_terms(flat, mods, nb, samples)
    term = lambda k: mods[pl.ds(k * width, width), :]
    qkv, att, mid, raised = take(), take(), take(), take()
    hidden = attention_part(
        state, patch, place, term, queries, mixes, qkv, att, mixed, raised, heads, samples, landed
    )
    drift = feed_part(
        hidden, state, term, out, scales, expands, shrinks, mid, mixed
    )
    results[0][...] = drift
    results[1][...] = drift.astype(BF16)
    for one in fetched:
        one.ready()


def run_network(fixed, pieces, sizes, nb, columns, heads, samples):
    width, tokens = fixed["place"].shape
    patch = fixed["state"].shape[0]
    ff = sizes[3] * width
    needs = ["terms", "state", "patch", "place", "out", "scales"]
    names = [name for name in needs if name in fixed]
    buffers, keys = [], []
    if pieces[0][0] is not None:
        pieces = sorted(pieces, key=lambda piece: (piece[0][0] != "p", piece[0][1:]))
    for key, rows, row in pieces:
        which = [k for k, known in enumerate(buffers) if known is rows]
        keys.append((key, which[0] if which else len(buffers), row))
        if not which:
            buffers.append(rows)
    operands = [fixed[name] for name in names] + buffers
    scratch = [pltpu.VMEM(rows.shape, rows.dtype) for rows in operands]
    scratch += [pltpu.VMEM((8 * width, tokens), F32), pltpu.VMEM((width, tokens), F32)]
    scratch += [
        pltpu.VMEM((3 * width, tokens), BF16),
        pltpu.VMEM((width, tokens), BF16),
        pltpu.VMEM((ff, tokens), BF16),
        pltpu.VMEM((heads * tokens // samples, tokens), F32),
    ]
    out_shape = [
        jax.ShapeDtypeStruct((patch, tokens), F32),
        jax.ShapeDtypeStruct((patch, tokens), BF16),
    ]
    if "terms" not in names:
        sources = 8 * width // columns
        out_shape.append(jax.ShapeDtypeStruct((sources * PAD, columns), F32))
    scratch.append(pltpu.SemaphoreType.DMA((len(operands),)))
    rows = 4 * width + 2 * ff
    return pl.pallas_call(
        functools.partial(
            network_kernel, names, keys, len(buffers), sizes, nb, heads, samples
        ),
        out_shape=out_shape,
        in_specs=[pl.BlockSpec(memory_space=pl.ANY)] * len(operands),
        out_specs=[pl.BlockSpec(memory_space=pltpu.VMEM)] * len(out_shape),
        scratch_shapes=scratch,
        compiler_params=pltpu.CompilerParams(vmem_limit_bytes=VMEM_LIMIT),
        cost_estimate=pl.CostEstimate(
            flops=2 * rows * width * tokens, bytes_accessed=2 * rows * width, transcendentals=0
        ),
    )(*operands)


def earlier_sum(value, narrow, count):
    position = lax.axis_index("tm")
    total = value
    before = jnp.zeros_like(value)
    low = 1
    while low < count:
        wide = low in (1, 4) and low * 2 < count
        distances = (low, 2 * low, 3 * low) if wide else (low,)
        others = [
            lax.ppermute(narrow, "tm", [(i, i ^ far) for i in range(count)]) for far in distances
        ]
        for far, other in zip(distances, others):
            other = other.astype(value.dtype)
            top = 2 * low if far > low else low
            before = jnp.where((position & top) != 0, before + other, before)
            total = total + other
        narrow = total.astype(BF16)
        low *= 4 if wide else 2
    return before


def body(
    noise,
    labels,
    timesteps,
    window_start,
    time_weight_in,
    time_weight_out,
    class_table,
    patch_weight,
    query_key_value,
    mix_weight,
    expand_weight,
    shrink_weight,
    block_modulation,
    final_modulation,
    output_weight,
):
    groups, count = lax.axis_size("group"), lax.axis_size("tm")
    samples, latent = noise.shape
    patch, width = patch_weight.shape
    each = latent // patch
    tokens = samples * each

    nq, nm, ne = query_key_value.shape[2], mix_weight.shape[2], expand_weight.shape[2]
    ns = shrink_weight.shape[1] // width
    columns = block_modulation.shape[2] + final_modulation.shape[1]
    packed = width // columns
    pack_rows = count * samples // max(packed, 1)
    sizes = (nq, nm, ne, ns, width, pack_rows)
    q_rows, m_rows, e_rows = query_key_value[0].T, mix_weight[0].T, expand_weight[0].T
    s_rows = shrink_weight[0].reshape(ns, width, nm).transpose(0, 2, 1)
    nb = block_modulation.shape[2]

    def prelude(times):
        return conditioning(
            times,
            window_start,
            labels,
            time_weight_in,
            time_weight_out,
            class_table,
            block_modulation[0].T,
            final_modulation.T,
            count,
        )

    place = jnp.asarray(position_columns(each, width, samples))
    part, scales = prelude(timesteps)
    start = noise.reshape(samples, each, patch).transpose(2, 0, 1).reshape(patch, tokens)
    fixed = dict(
        scales=scales, patch=patch_weight.T, place=place, out=output_weight.T, state=start
    )

    def network(pieces, **more):
        return run_network({**fixed, **more}, pieces, sizes, nb, columns, HEADS, samples)

    short = (
        groups == 2
        and count == 16
        and ns % 2 == 0
        and packed * columns == width
        and packed * pack_rows == count * samples
        and samples <= PAD
        and all(v % 16 == 0 for v in (nq, nm, ne // 2, pack_rows))
    )
    if short:
        half_e, half_s = ne // 2, ns // 2
        packs = [part[k * pack_rows : (k + 1) * pack_rows] for k in range(packed)]
        packs = jnp.concatenate(packs, axis=1).astype(BF16)
        first = jnp.concatenate([q_rows, m_rows, packs], axis=0)
        halves = [
            jnp.concatenate(
                [e_rows[k * half_e : (k + 1) * half_e]]
                + [s_rows[k * half_s + j] for j in range(half_s)],
                axis=0,
            )
            for k in range(2)
        ]
        pieces = spread_weights(first, halves, groups, count, ORDER)
        drift, narrow, terms = network(pieces)
    else:
        whole = lambda rows, axis: lax.all_gather(rows, "tm", axis=axis, tiled=True)
        terms = part.astype(BF16).reshape(count, samples, columns)
        terms = lax.all_to_all(terms, "tm", split_axis=0, concat_axis=0, tiled=True)
        terms = jnp.pad(terms.astype(F32), ((0, 0), (0, -samples % PAD), (0, 0)))
        terms = terms.reshape(count * PAD, columns)
        pieces = [
            (None, whole(q_rows, 0), 0),
            (None, whole(m_rows, 0), 0),
            (None, whole(e_rows, 0), 0),
            (None, whole(s_rows, 1).reshape(ns * width, width), 0),
        ]
        drift, narrow = network(pieces, terms=terms)

    states = start
    for sweep in range(ITERS):
        if sweep > 0:
            drift, narrow = network(pieces, terms=terms, state=states)
        before = earlier_sum(drift, narrow, count)
        running = before + drift
        states = start + before
    result = (start + running).reshape(patch, samples, each).transpose(1, 2, 0)
    return result.reshape(1, samples, latent)


def solution(mesh):
    return jax.shard_map(
        body,
        mesh=mesh,
        in_specs=(
            P("group", None),
            P("group"),
            P(),
            P(),
            P(),
            P(),
            P(),
            P(),
            P(None, None, "tm"),
            P(None, None, "tm"),
            P(None, None, "tm"),
            P(None, None, "tm"),
            P(None, None, "tm"),
            P(None, "tm"),
            P(),
        ),
        out_specs=P("tm", "group", None),
        check_vma=False,
    )
```
